256 devices in a mesh: dom: 64 (over y_hi, x, z), cls: 4 (over y_lo, core).
Axes of the slice: x: 4, y: 4 (y_hi: 2, y_lo: 2; y = y_hi * 2 + y_lo), z: 8, core: 2. Of those that a mesh axis runs over, the one named last changes fastest.
Arguments:
- particles: bfloat16 [4096, 2, 2048], P('dom'), may hold values from -8 to 8
- offsets: int32 [4096, 2], P('dom'), may hold values from -3 to 3
- ref_maps: bfloat16 [8, 4096, 2, 2048], P('cls', 'dom'), may hold values from -0.15 to 0.15
- inv_sigma2: float32 [2048], replicated, may hold values from 0.3 to 3
- log_prior: float32 [8], P('cls'), may hold values from -1.5 to 0
- orient: int32 [2, 64], P(None, 'dom'), may hold values from 0 to 63
Outputs:
- slice_sums: float32 [2, 8, 64, 2, 2048], P(None, 'cls', 'dom')
- weight_sums: float32 [2, 8, 64], P(None, 'cls', 'dom')
- particle_loglik: float32 [2, 4096], P(None, 'dom')
The draws below stay inside these ranges and needn't reach their ends.
All inputs are finite; a program needn't handle non-finite values.
Results may differ from the reference program's by a relative error of at most 0.0019.
The reference program's roundings to bfloat16 on the way (of `picked`, `weighted`, `shifted` and `posterior`) count: a program that leaves them out, or rounds other values in their place, can miss the bound.
Values may be sent and summed in bfloat16 or wider, within the bound.
A program may use at most 128 MiB of HBM per device.

```python
import math
import jax
import jax.numpy as jnp
from jax import lax

BOX = 256
K = 8
KYW = 128
FPIX = 2048
N_DEV = 64
NPART = 4096
R_DEV = 64
RTOT = 4096
OR_DEV = 1
NOR = 64
ROUNDS = 2


def common_maps(key):
    signs = jax.random.bernoulli(key, 0.5, (2, FPIX)).astype(jnp.float32)
    return 0.1 * (2.0 * signs - 1.0)


def draw_ref_maps(key, part):
    base_key = key
    key = jax.random.fold_in(key, 11)
    noise = jax.random.normal(key, (K, RTOT, 2, FPIX), jnp.float32)
    values = common_maps(base_key)[None, None] + 0.03 * noise
    return jnp.clip(values, -0.149, 0.149).astype(jnp.bfloat16)


def draw_particles(key, part):
    base_key = key
    key = jax.random.fold_in(key, 12)
    keys = jax.random.split(key, 4)
    aligned = (jax.random.randint(keys[3], (NPART,), 0, 8) == 0).astype(jnp.float32)
    strength = jax.random.uniform(keys[2], (NPART,), jnp.float32, 70.0, 80.0)
    noise = jax.random.normal(keys[0], (NPART, 2, FPIX), jnp.float32)
    values = noise + (aligned * strength)[:, None, None] * common_maps(base_key)[None]
    return jnp.clip(values, -8.0, 8.0).astype(jnp.bfloat16)


def with_ends(drawn, stream_key, least, high):
    extent = drawn.shape
    place = [jax.random.randint(jax.random.fold_in(stream_key, axis), (), 0, extent[axis]) for axis in range(len(extent))]
    drawn = drawn.at[tuple(place)].set(least)
    longest = extent.index(max(extent))
    place[longest] = (place[longest] + 1) % extent[longest]
    return drawn.at[tuple(place)].set(high)


def level_of(rng, extent, cuts, low, largest):
    def one(axis_at, parts):
        steps = jax.random.uniform(jax.random.fold_in(jax.random.fold_in(rng, 6), axis_at), (parts,), jnp.float32, low / len(cuts), largest / len(cuts))
        return jnp.repeat(jnp.exp(steps), extent[axis_at] // parts).reshape((-1,) + (1,) * (len(extent) - axis_at - 1))

    level = one(*cuts[0])
    for cut in cuts[1:]:
        level = level * one(*cut)
    return level


def setup_inputs(seed: int = 0) -> dict:
    splits = jax.random.split(jax.random.key(seed), 7)
    particles = draw_particles(jax.random.fold_in(splits[6], 71), 0)
    offsets = with_ends(jax.random.randint(splits[1], (NPART, 2), -3, 4), jax.random.fold_in(splits[1], 1), -3, 3).astype(jnp.int32)
    ref_maps = draw_ref_maps(jax.random.fold_in(splits[6], 71), 0)
    inv_sigma2 = jnp.clip(jnp.exp(jax.random.uniform(splits[3], (FPIX,), jnp.float32, math.log(0.3), math.log(3.0))), 0.3, 3.0)
    log_prior = jnp.clip(-1.5 + 1.5 * jax.random.uniform(splits[4], (K,), jnp.float32) ** level_of(splits[4], (K,), ((0, 4),), -0.2, 0.2), -1.5, 0.0)
    orient = with_ends(jax.random.randint(splits[5], (ROUNDS, NOR), 0, R_DEV), jax.random.fold_in(splits[5], 1), 0, R_DEV - 1).astype(jnp.int32)
    return dict(particles=particles, offsets=offsets, ref_maps=ref_maps, inv_sigma2=inv_sigma2, log_prior=log_prior, orient=orient)


def shift_block(particles, offsets, step_y):
    particle_count = particles.shape[0]
    pixels = jnp.arange(FPIX, dtype=jnp.int32)
    freq_x = pixels // KYW
    freq_y = pixels % KYW - KYW // 2
    step_x = jnp.arange(5, dtype=jnp.int32) - 2
    shift_x = offsets[:, 0:1] + step_x[None, :]
    shift_y = offsets[:, 1:2] + step_y
    phase_turns = jnp.mod(shift_x[:, :, None] * freq_x[None, None, :] + shift_y[:, :, None] * freq_y[None, None, :], BOX)
    angles = phase_turns.astype(jnp.float32) * (2.0 * math.pi / BOX)
    cosine_part = jnp.cos(angles)
    sine_part = jnp.sin(angles)
    real_part = particles[:, 0, :].astype(jnp.float32)[:, None, :]
    imag_part = particles[:, 1, :].astype(jnp.float32)[:, None, :]
    shifted = jnp.stack([real_part * cosine_part + imag_part * sine_part, imag_part * cosine_part - real_part * sine_part], axis=2)
    return shifted.astype(jnp.bfloat16).reshape(particle_count * 5, 2 * FPIX)


def score_pass(particles, offsets, weighted, bias_terms):
    particle_count = particles.shape[0]
    columns = weighted.shape[0]
    score_rows = []
    for step_y in range(-2, 3):
        shifted = shift_block(particles, offsets, step_y)
        score_rows.append(jnp.dot(shifted, weighted.T, preferred_element_type=jnp.float32).reshape(particle_count, 5, columns))
    return jnp.stack(score_rows, axis=1) + bias_terms


def back_pass(particles, offsets, posterior):
    particle_count = particles.shape[0]
    columns = posterior.shape[-1]
    accumulated = jnp.zeros((columns, 2 * FPIX), jnp.float32)
    for block_index, step_y in enumerate(range(-2, 3)):
        shifted = shift_block(particles, offsets, step_y)
        post_rows = posterior[:, block_index].reshape(particle_count * 5, columns)
        accumulated = accumulated + jnp.dot(post_rows.T, shifted, preferred_element_type=jnp.float32)
    return accumulated


def reference(particles, offsets, ref_maps, inv_sigma2, log_prior, orient):
    row_width = 2 * FPIX
    noise_weight = jnp.concatenate([inv_sigma2, inv_sigma2])
    blocks = NPART // N_DEV
    part_blocks = particles.reshape(blocks, N_DEV, 2, FPIX)
    offset_blocks = offsets.reshape(blocks, N_DEV, 2)
    slice_list = []
    weight_list = []
    loglik_list = []
    for round_index in range(ROUNDS):
        grid_rows = (jnp.arange(NOR, dtype=jnp.int32) // OR_DEV) * R_DEV + orient[round_index].astype(jnp.int32)
        picked = ref_maps[:, grid_rows].reshape(K, NOR, row_width).astype(jnp.float32)
        weighted = (picked * noise_weight).astype(jnp.bfloat16).reshape(K * NOR, row_width)
        energy = 0.5 * jnp.sum(picked * picked * noise_weight, axis=-1)
        bias_terms = (log_prior[:, None] - energy).reshape(K * NOR)

        def visit_block(running, inputs):
            block, block_offsets = inputs
            logits = score_pass(block, block_offsets, weighted, bias_terms)
            maximum = jnp.max(logits, axis=(1, 2, 3))
            partition = jnp.sum(jnp.exp(logits - maximum[:, None, None, None]), axis=(1, 2, 3))
            posterior = (jnp.exp(logits - maximum[:, None, None, None]) / partition[:, None, None, None]).astype(jnp.bfloat16)
            slice_total = running[0] + back_pass(block, block_offsets, posterior)
            weight_total = running[1] + jnp.sum(posterior.astype(jnp.float32), axis=(0, 1, 2))
            return (slice_total, weight_total), maximum + jnp.log(partition)

        initial = (jnp.zeros((K * NOR, row_width), jnp.float32), jnp.zeros((K * NOR,), jnp.float32))
        (slice_total, weight_total), logliks = lax.scan(visit_block, initial, (part_blocks, offset_blocks))
        slice_list.append(slice_total.reshape(K, NOR, 2, FPIX))
        weight_list.append(weight_total.reshape(K, NOR))
        loglik_list.append(logliks.reshape(NPART))
    return jnp.stack(slice_list, axis=0), jnp.stack(weight_list, axis=0), jnp.stack(loglik_list, axis=0)
```

```python
import math

import jax
import jax.numpy as jnp
import numpy as np
from jax import lax
from jax.experimental import pallas as pl
from jax.experimental.pallas import tpu as pltpu
from jax.sharding import PartitionSpec as P

MESH = pl.DeviceIdType.MESH
BOX = 256
KYW = 128
FPIX = 2048
XN = 4
ZN = 8
HALF = 32
STEPS = 25
ROWS = 1792
LIVE = 1600
WIDTH = 2 * FPIX + 128
PACK = 1152
GCUT = 640
SUMW = 128 + FPIX
SCUT = 1152
DELTA = (0, -1, 1, -2, 2, -3, 3, -4)
ORDER = (4, -3, 3, -2, 2, -1, 1, 0)


def tables():
    table = np.zeros((17, 8, 128), np.float64)
    for step in (1, 2, 3):
        for kx in range(16):
            turn = 2.0 * math.pi * ((kx * step) % BOX) / BOX
            table[kx, 2 * step - 2] = math.cos(turn)
            table[kx, 2 * step - 1] = math.sin(turn)
        ky = np.arange(KYW) - KYW // 2
        turn = 2.0 * math.pi * ((ky * step) % BOX) / BOX
        table[16, 2 * step - 2] = np.cos(turn)
        table[16, 2 * step - 1] = np.sin(turn)
    return table.astype(np.float32)


def by_offset(offset, row):
    size = jnp.abs(offset)
    cosine = jnp.where(
        size < 0.5, 1.0, jnp.where(size < 1.5, row[0:1], jnp.where(size < 2.5, row[2:3], row[4:5]))
    )
    sine = jnp.where(
        size < 0.5, 0.0, jnp.where(size < 1.5, row[1:2], jnp.where(size < 2.5, row[3:4], row[5:6]))
    )
    return cosine, jnp.where(offset < 0, -sine, sine)


def rotations(real, imag, row):
    result = [None] * 5
    result[2] = (real, imag)
    for step in (1, 2):
        cosine, sine = row[2 * step - 2 : 2 * step - 1], row[2 * step - 1 : 2 * step]
        rc, rs, ic, is_ = real * cosine, real * sine, imag * cosine, imag * sine
        result[2 + step] = (rc + is_, ic - rs)
        result[2 - step] = (rc - is_, ic + rs)
    return result


def kernel(
    orient, prior, noise, table, offsets, particles, maps,
    sums_out, counts_out, loglik_out,
    block, given, gath, pix, offs, base, shifted, weights, logits, post, stats,
    part, sib, outr, llr,
    ax_l, ax_r, ax_f, az_p, az_m, b_p, b_m, bx_l, bx_r, bx_f,
    s_swap, r_swap, s_pix, r_pix, s_st, r_st, s_out, r_out, s_ll, r_ll,
    s_zp, r_zp, s_zm, r_zm, s_xr, r_xr, s_xl, r_xl, s_xf, r_xf, s_sd, r_sd,
    s_y, r_y, s_wp, r_wp, s_wm, r_wm, s_se, r_se,
    s_d2, r_d2, s_al, r_al, s_ar, r_ar, s_af, r_af, s_ap, r_ap, s_am, r_am,
    s_bp, r_bp, s_bm, r_bm, s_bx, r_bx,
):
    dom, cls = lax.axis_index("dom"), lax.axis_index("cls")
    y_hi, x, z = lax.div(dom, 32), lax.rem(lax.div(dom, 8), XN), lax.rem(dom, ZN)
    y_lo, core = lax.div(cls, 2), lax.rem(cls, 2)
    y = y_hi * 2 + y_lo

    def device(yy, cc, xx, zz):
        return ((lax.div(yy, 2) * XN + xx) * ZN + zz, lax.rem(yy, 2) * 2 + cc)

    def xat(d):
        return lax.rem(x + (XN + d), XN)

    def zat(d):
        return lax.rem(z + (ZN + d), ZN)

    def yat(d):
        return lax.rem(y + d, 4)

    x_up, x_down = device(y, core, xat(1), z), device(y, core, xat(-1), z)
    z_up, z_down = device(y, core, x, zat(1)), device(y, core, x, zat(-1))
    sibling = device(y, 1 - core, x, z)
    across = device(yat(2), 1 - core, x, z)
    mate = device(3 - y, core, x, z)
    y_peers = [device(yat(d), core, x, z) for d in (1, 2, 3)]
    foreign = y_hi != core

    def send(src, dst, ssem, rsem, to):
        copy = pltpu.make_async_remote_copy(
            src_ref=src, dst_ref=dst, send_sem=ssem, recv_sem=rsem, device_id=to, device_id_type=MESH
        )
        copy.start()

    def landed(dst, rsem):
        pltpu.make_async_copy(dst, dst, rsem).wait()

    def left(src, ssem):
        pltpu.make_async_copy(src, src, ssem).wait()

    barrier = pltpu.get_barrier_semaphore()
    for other in [x_up, x_down, z_up, z_down, sibling, across] + y_peers:
        pl.semaphore_signal(barrier, inc=1, device_id=other, device_id_type=MESH)

    lane = lax.broadcasted_iota(jnp.int32, (1, 128), 1)
    weight = noise[...]
    for r in range(2):
        for k in range(2):
            picked = maps[k, orient[r, 0]].astype(jnp.float32)
            scaled = picked * weight
            energy = 0.5 * jnp.sum(jnp.sum(scaled * picked, axis=0, keepdims=True), axis=1, keepdims=True)
            bias = prior[k] - energy
            high = bias.astype(jnp.bfloat16).astype(jnp.float32)
            rest = bias - high
            middle = rest.astype(jnp.bfloat16).astype(jnp.float32)
            low = rest - middle
            row = 2 * r + k
            for q in range(4):
                block[q * 4 + row : q * 4 + row + 1, 0:1024] = scaled[
                    q // 2 : q // 2 + 1, (q % 2) * 1024 : (q % 2) * 1024 + 1024
                ]
                block[q * 4 + row : q * 4 + row + 1, 1024:PACK] = jnp.where(
                    lane == 0, high, jnp.where(lane == 1, middle, jnp.where(lane == 2, low, 0.0))
                )
    given[...] = block[...].astype(jnp.bfloat16)

    first = pl.multiple_of(core * HALF, HALF)
    mine = pl.ds(first, HALF)

    @pl.loop(0, 16)
    def _(tile):
        lanes = pl.ds(pl.multiple_of(tile * 128, 128), 128)
        both = particles[mine, :, lanes].astype(jnp.float32)
        pix[y_hi, 0, :, lanes] = both[:, 0, :].astype(jnp.bfloat16)
        pix[y_hi, 1, :, lanes] = both[:, 1, :].astype(jnp.bfloat16)

    both = offsets[mine, :]
    offs[y_hi] = jnp.where(lane == 0, both[:, 0:1], both[:, 1:2])

    pl.semaphore_wait(barrier, 9)

    own = gath.at[core, z, x]

    @pl.when(foreign)
    def _():
        send(given, gath.at[y_hi, z, x], s_swap, r_swap, across)

    @pl.when(jnp.logical_not(foreign))
    def _():
        own[...] = given[...]

    send(pix.at[y_hi], pix.at[y_hi], s_pix.at[0], r_pix.at[0], mate)
    send(offs.at[y_hi], offs.at[y_hi], s_pix.at[1], r_pix.at[1], mate)

    @pl.when(foreign)
    def _():
        landed(own, r_swap)
        left(given, s_swap)

    ca, cb = pl.ds(0, GCUT), pl.ds(GCUT, PACK - GCUT)

    def ga(dz, dx):
        return gath.at[core, zat(dz), xat(dx), :, ca]

    def gb(dz, dx):
        return gath.at[core, zat(dz), xat(dx), :, cb]

    def ga_row(dz, c=None):
        return gath.at[core if c is None else c, zat(dz), :, :, ca]

    def gb_row(dz, c=None):
        return gath.at[core if c is None else c, zat(dz), :, :, cb]

    def zp(s):
        send(ga(1 - s, 0), ga(1 - s, 0), s_zp.at[s - 1], r_zp.at[s - 1], z_up)

    def zm(s):
        send(ga(s - 1, 0), ga(s - 1, 0), s_zm.at[s - 1], r_zm.at[s - 1], z_down)

    def xs(j):
        ref = ga(DELTA[j], 0)
        send(ref, ref, s_xr.at[j], r_xr.at[j], x_up)
        send(ref, ref, s_xl.at[j], r_xl.at[j], x_down)

    def wait_zp(s):
        landed(ga(-s, 0), r_zp.at[s - 1])

    def wait_zm(s):
        landed(ga(s, 0), r_zm.at[s - 1])

    def far(j):
        landed(ga(DELTA[j], -1), r_xr.at[j])
        if j % 2 == 0:
            ref = ga(DELTA[j], -1)
            send(ref, ref, s_xf.at[j], r_xf.at[j], x_up)
        landed(ga(DELTA[j], 1), r_xl.at[j])
        if j % 2 == 1:
            ref = ga(DELTA[j], 1)
            send(ref, ref, s_xf.at[j], r_xf.at[j], x_down)

    def row_a(j):
        landed(ga(DELTA[j], 2), r_xf.at[j])
        send(ga_row(DELTA[j]), ga_row(DELTA[j]), s_sd.at[j], r_sd.at[j], sibling)

    def wp(s):
        send(gb_row(1 - s), gb_row(1 - s), s_wp.at[s - 1], r_wp.at[s - 1], z_up)

    def wm(s):
        send(gb_row(s - 1), gb_row(s - 1), s_wm.at[s - 1], r_wm.at[s - 1], z_down)

    def row_b(j):
        send(gb_row(DELTA[j]), gb_row(DELTA[j]), s_se.at[j], r_se.at[j], sibling)

    def wait_wp(s):
        landed(gb_row(-s), r_wp.at[s - 1])

    def wait_wm(s):
        landed(gb_row(s), r_wm.at[s - 1])

    def prepare(h):
        both = offs[h].astype(jnp.float32)
        base[0] = jnp.broadcast_to(both[:, 0:1], (HALF, 128))
        cosine, sine = by_offset(jnp.broadcast_to(both[:, 1:2], (HALF, 128)), table[16])
        base[1] = cosine
        base[2] = sine

    def shift(h, begin, end):
        @pl.loop(begin, end)
        def _(kx):
            start = pl.multiple_of(kx * 128, 128)
            row = table[kx]
            for g in range(0, HALF, 16):
                real = pix[h, 0, g : g + 16, pl.ds(start, 128)].astype(jnp.float32)
                imag = pix[h, 1, g : g + 16, pl.ds(start, 128)].astype(jnp.float32)
                cx, sx = by_offset(base[0, g : g + 16], row)
                cy, sy = base[1, g : g + 16], base[2, g : g + 16]
                cosine, sine = cx * cy - sx * sy, sx * cy + cx * sy
                real, imag = real * cosine + imag * sine, imag * cosine - real * sine
                for iy, (ry, iy_) in enumerate(rotations(real, imag, table[16])):
                    for ix, (rx, im) in enumerate(rotations(ry, iy_, row)):
                        at = pl.ds(pl.multiple_of((iy * 5 + ix) * 64 + g + h * HALF, 16), 16)
                        shifted[at, pl.ds(start, 128)] = rx.astype(jnp.bfloat16)
                        shifted[at, pl.ds(pl.multiple_of(start + FPIX, 128), 128)] = im.astype(jnp.bfloat16)

    zp(1)
    zm(1)
    send(gb(0, 0), gb(0, 0), s_y.at[0], r_y.at[0], x_up)
    send(gb(0, 0), gb(0, 0), s_y.at[1], r_y.at[1], x_down)
    xs(0)
    prepare(y_hi)
    shift(y_hi, 0, 2)
    landed(gb(0, -1), r_y.at[0])
    send(gb(0, -1), gb(0, -1), s_y.at[2], r_y.at[2], x_up)
    wait_zp(1)
    zp(2)
    xs(1)
    wait_zm(1)
    zm(2)
    xs(2)
    landed(gb(0, 1), r_y.at[1])
    far(0)
    shift(y_hi, 2, 4)
    landed(gb(0, 2), r_y.at[2])
    wp(1)
    wm(1)
    row_b(0)
    wait_zp(2)
    zp(3)
    xs(3)
    wait_zm(2)
    zm(3)
    xs(4)
    shift(y_hi, 4, 6)
    far(1)
    row_a(0)
    wait_wp(1)
    wp(2)
    wait_wm(1)
    wm(2)
    far(2)
    shift(y_hi, 6, 8)
    wait_zp(3)
    zp(4)
    xs(5)
    wait_zm(3)
    xs(6)
    row_b(1)
    row_b(2)
    row_a(1)
    shift(y_hi, 8, 10)
    wait_wp(2)
    wp(3)
    wait_wm(2)
    wm(3)
    far(3)
    far(4)
    wait_zp(4)
    xs(7)
    row_b(3)
    row_b(4)
    row_a(2)
    shift(y_hi, 10, 12)
    far(5)
    wait_wm(3)
    wm(4)
    wait_wp(3)
    row_b(6)
    row_b(5)
    row_a(3)
    far(6)
    shift(y_hi, 12, 14)
    row_a(4)
    far(7)
    row_a(5)
    shift(y_hi, 14, 16)
    row_a(6)
    row_a(7)

    wide = lax.broadcasted_iota(jnp.int32, (LIVE, 128), 1)
    shifted[0:LIVE, 2 * FPIX : WIDTH] = jnp.where(wide < 3, 1.0, 0.0).astype(jnp.bfloat16)
    shifted[LIVE:ROWS, :] = jnp.zeros((ROWS - LIVE, WIDTH), jnp.bfloat16)
    post[:, LIVE + 64 : ROWS] = jnp.zeros((256, ROWS - LIVE - 64), jnp.bfloat16)

    landed(pix.at[1 - y_hi], r_pix.at[0])
    landed(offs.at[1 - y_hi], r_pix.at[1])
    prepare(1 - y_hi)
    shift(1 - y_hi, 0, 16)

    wait_wm(4)
    row_b(7)
    for j in range(8):
        landed(ga_row(DELTA[j], 1 - core), r_sd.at[j])
        landed(gb_row(DELTA[j], 1 - core), r_se.at[j])

    upper = lax.broadcasted_iota(jnp.int32, (8, 1024), 0) < 4

    @pl.loop(0, 16)
    def _(group):
        gb_, gz = lax.div(group, 8), lax.rem(group, 8)
        rows = pl.ds(pl.multiple_of(group * 16, 16), 16)
        tiles = [gath[gb_, gz, i].astype(jnp.float32) for i in range(4)]
        for t in range(2):
            t0, t1, t2, t3 = [tile[8 * t : 8 * t + 8, 0:1024] for tile in tiles]
            weights[rows, 2048 * t : 2048 * t + 1024] = jnp.concatenate(
                [jnp.where(upper, t0, pltpu.roll(t1, 4, 0)), jnp.where(upper, t2, pltpu.roll(t3, 4, 0))], axis=0
            ).astype(jnp.bfloat16)
            weights[rows, 2048 * t + 1024 : 2048 * t + 2048] = jnp.concatenate(
                [jnp.where(upper, pltpu.roll(t0, 4, 0), t1), jnp.where(upper, pltpu.roll(t2, 4, 0), t3)], axis=0
            ).astype(jnp.bfloat16)
        t0, t1, t2, t3 = [tile[0:8, 1024:PACK] for tile in tiles]
        up = upper[:, 0:128]
        weights[rows, 2 * FPIX : WIDTH] = jnp.concatenate(
            [jnp.where(up, t0, pltpu.roll(t1, 4, 0)), jnp.where(up, t2, pltpu.roll(t3, 4, 0))], axis=0
        ).astype(jnp.bfloat16)

    @pl.loop(0, 7)
    def _(tile):
        at = pl.ds(pl.multiple_of(tile * 256, 256), 256)
        logits[:, at] = lax.dot_general(
            weights[...], shifted[at, :], (((1,), (1,)), ((), ())), preferred_element_type=jnp.float32
        )

    sub = lax.broadcasted_iota(jnp.int32, (8, 128), 0)

    def over_group(value, join):
        value = join(value, pltpu.roll(value, 4, 0))
        value = join(value, jnp.where(sub % 2 == 0, pltpu.roll(value, 7, 0), pltpu.roll(value, 1, 0)))
        return join(value, pltpu.roll(value, 64, 1))

    live = lax.broadcasted_iota(jnp.int32, (256, 128), 1) < 64
    last = pl.ds(LIVE - 64, 128)
    logits[:, last] = jnp.where(live, logits[:, last], -3.0e38)

    def peak_of(tile, carry):
        at = pl.ds(pl.multiple_of(tile * 128, 128), 128)
        return jnp.maximum(carry, jnp.max(logits[:, at].reshape(32, 8, 128), axis=0))

    peak = over_group(lax.fori_loop(0, 13, peak_of, jnp.full((8, 128), -3.0e38, jnp.float32)), jnp.maximum)

    def total_of(tile, carry):
        at = pl.ds(pl.multiple_of(tile * 128, 128), 128)
        value = jnp.exp(logits[:, at].reshape(32, 8, 128) - peak[None])
        logits[:, at] = value.reshape(256, 128)
        return carry + jnp.sum(value, axis=0)

    total = over_group(lax.fori_loop(0, 13, total_of, jnp.zeros((8, 128), jnp.float32)), jnp.add)

    stats[y, 0] = peak
    stats[y, 1] = total
    for i in range(3):
        send(stats.at[y], stats.at[y], s_st.at[i], r_st.at[i], y_peers[i])
    for i in range(3):
        landed(stats.at[yat(3 - i)], r_st.at[i])
    peaks = [stats[i, 0] for i in range(4)]
    top = jnp.maximum(jnp.maximum(peaks[0], peaks[1]), jnp.maximum(peaks[2], peaks[3]))
    whole = stats[0, 1] * jnp.exp(peaks[0] - top)
    for i in range(1, 4):
        whole = whole + stats[i, 1] * jnp.exp(peaks[i] - top)
    scale = jnp.exp(peak - top) / whole
    llr[core] = top + jnp.log(whole)
    send(llr.at[core], llr.at[core], s_ll, r_ll, sibling)

    @pl.loop(0, 13)
    def _(tile):
        at = pl.ds(pl.multiple_of(tile * 128, 128), 128)
        value = logits[:, at].reshape(32, 8, 128) * scale[None]
        post[:, at] = value.reshape(256, 128).astype(jnp.bfloat16)

    def product(at):
        return jnp.dot(post[...], shifted[:, at], preferred_element_type=jnp.float32)

    def store(at, top_, bottom, width):
        keep = lax.broadcasted_iota(jnp.int32, (256, width), 0) % 8 < 4
        even = jnp.where(keep, top_, pltpu.roll(bottom, 4, 0))
        odd = jnp.where(keep, pltpu.roll(top_, 252, 0), bottom)
        part[:, 0, :, at] = even.reshape(32, 8, width)
        part[:, 1, :, at] = odd.reshape(32, 8, width)

    def trade(at, i):
        send(part.at[pl.ds((1 - core) * 16, 16), :, :, at], sib.at[:, :, :, at], s_d2.at[i], r_d2.at[i], sibling)

    def collect(at, i):
        landed(sib.at[:, :, :, at], r_d2.at[i])

        @pl.loop(0, 16)
        def _(pair):
            row = core * 16 + pair
            part[row, :, :, at] = part[row, :, :, at] + sib[pair, :, :, at]

    edge = product(pl.ds(2 * FPIX, 128))
    store(pl.ds(0, 128), edge, edge, 128)
    for j in range(4):
        store(
            pl.ds(128 + 512 * j, 512), product(pl.ds(512 * j, 512)), product(pl.ds(FPIX + 512 * j, 512)), 512
        )
        if j == 1:
            trade(pl.ds(0, SCUT), 0)
        if j == 3:
            trade(pl.ds(SCUT, SUMW - SCUT), 1)

    sa, sb = pl.ds(0, SCUT), pl.ds(SCUT, SUMW - SCUT)

    def pa(dz, dx, at):
        xx = xat(dx)
        return part.at[core * 16 + zat(dz) * 2 + lax.div(xx, 2), lax.rem(xx, 2), :, at]

    def add(dst, src):
        dst[...] = dst[...] + src[...]

    def a_start(i):
        d = ORDER[i]
        if i % 2 == 0:
            send(pa(d, 2, sa), ax_f.at[i], s_af.at[i], r_af.at[i], x_up)
            send(pa(d, -1, sa), ax_r.at[i], s_ar.at[i], r_ar.at[i], x_down)
        else:
            send(pa(d, 2, sa), ax_f.at[i], s_af.at[i], r_af.at[i], x_down)
            send(pa(d, 1, sa), ax_l.at[i], s_al.at[i], r_al.at[i], x_up)

    def a_far(i):
        d = ORDER[i]
        landed(ax_f.at[i], r_af.at[i])
        if i % 2 == 0:
            add(ax_f.at[i], pa(d, 1, sa))
            send(ax_f.at[i], ax_l.at[i], s_al.at[i], r_al.at[i], x_up)
        else:
            add(ax_f.at[i], pa(d, -1, sa))
            send(ax_f.at[i], ax_r.at[i], s_ar.at[i], r_ar.at[i], x_down)

    def a_sum(i):
        own_ = pa(ORDER[i], 0, sa)
        landed(ax_l.at[i], r_al.at[i])
        landed(ax_r.at[i], r_ar.at[i])
        own_[...] = own_[...] + ax_l[i] + ax_r[i]
        if i == 0:
            send(own_, az_p.at[0], s_ap.at[0], r_ap.at[0], z_up)
        elif i == 1:
            send(own_, az_m.at[0], s_am.at[0], r_am.at[0], z_down)
        elif i < 7 and i % 2 == 0:
            s = i // 2
            landed(az_p.at[s - 1], r_ap.at[s - 1])
            add(az_p.at[s - 1], own_)
            send(az_p.at[s - 1], az_p.at[s], s_ap.at[s], r_ap.at[s], z_up)
        elif i < 7:
            s = i // 2
            landed(az_m.at[s - 1], r_am.at[s - 1])
            add(az_m.at[s - 1], own_)
            send(az_m.at[s - 1], az_m.at[s], s_am.at[s], r_am.at[s], z_down)
        else:
            landed(az_p.at[3], r_ap.at[3])
            landed(az_m.at[2], r_am.at[2])
            own_[...] = own_[...] + az_p[3] + az_m[2]

    XREL = (2, 1, -1, 0)

    def b_start(c):
        send(pa(-4, XREL[c], sb), b_m.at[c, 0], s_bm.at[c, 0], r_bm.at[c, 0], z_down)
        send(pa(3, XREL[c], sb), b_p.at[c, 0], s_bp.at[c, 0], r_bp.at[c, 0], z_up)

    def b_step(s, c):
        landed(b_m.at[c, s - 1], r_bm.at[c, s - 1])
        add(b_m.at[c, s - 1], pa(-4 + s, XREL[c], sb))
        send(b_m.at[c, s - 1], b_m.at[c, s], s_bm.at[c, s], r_bm.at[c, s], z_down)
        if s < 3:
            landed(b_p.at[c, s - 1], r_bp.at[c, s - 1])
            add(b_p.at[c, s - 1], pa(3 - s, XREL[c], sb))
            send(b_p.at[c, s - 1], b_p.at[c, s], s_bp.at[c, s], r_bp.at[c, s], z_up)

    def b_sum(c):
        own_ = pa(0, XREL[c], sb)
        landed(b_m.at[c, 3], r_bm.at[c, 3])
        landed(b_p.at[c, 2], r_bp.at[c, 2])
        own_[...] = own_[...] + b_m[c, 3] + b_p[c, 2]
        if c == 0:
            send(own_, bx_f, s_bx.at[0], r_bx.at[0], x_up)
        elif c == 1:
            landed(bx_f, r_bx.at[0])
            add(bx_f, own_)
            send(bx_f, bx_l, s_bx.at[1], r_bx.at[1], x_up)
        elif c == 2:
            send(own_, bx_r, s_bx.at[2], r_bx.at[2], x_down)
        else:
            landed(bx_l, r_bx.at[1])
            landed(bx_r, r_bx.at[2])
            own_[...] = own_[...] + bx_l[...] + bx_r[...]

    collect(pl.ds(0, SCUT), 0)
    for i in range(8):
        a_start(i)
    collect(pl.ds(SCUT, SUMW - SCUT), 1)
    for c in range(4):
        b_start(c)
    a_far(0)
    a_far(1)
    for c in range(4):
        b_step(1, c)
        a_far(2 + c)
    a_sum(0)
    a_sum(1)
    a_far(6)
    b_step(2, 0)
    b_step(2, 1)
    a_far(7)
    b_step(2, 2)
    b_step(2, 3)
    a_sum(2)
    a_sum(3)
    b_step(3, 0)
    b_step(3, 1)
    a_sum(4)
    b_step(3, 2)
    b_step(3, 3)
    a_sum(5)
    b_sum(0)
    b_sum(1)
    a_sum(6)
    b_sum(2)
    b_sum(3)
    a_sum(7)

    done = part.at[core * 16 + z * 2 + lax.div(x, 2), lax.rem(x, 2)]

    @pl.when(foreign)
    def _():
        send(done, outr, s_out, r_out, across)
        left(done, s_out)
        landed(outr, r_out)

    @pl.when(jnp.logical_not(foreign))
    def _():
        outr[...] = done[...]

    counts_out[...] = outr[:, 0:128]
    sums_out[...] = outr[:, 128:SUMW]

    landed(llr.at[1 - core], r_ll)

    loglik_out[...] = jnp.where(
        lax.broadcasted_iota(jnp.int32, (8, 128), 1) < 32,
        jnp.where(y_hi == 0, llr[0], pltpu.roll(llr[0], 96, 1)),
        jnp.where(y_hi == 1, llr[1], pltpu.roll(llr[1], 32, 1)),
    )

    left(pix.at[0], s_pix.at[0])
    left(offs.at[0], s_pix.at[1])
    left(llr.at[0], s_ll)
    for i in range(3):
        left(stats.at[0], s_st.at[i])
        left(gb(0, 0), s_y.at[i])
        left(gb_row(0), s_wp.at[i])
        left(ga(0, 0), s_zm.at[i])
        left(az_m.at[0], s_am.at[i])
        left(bx_f, s_bx.at[i])
    for i in range(4):
        left(gb_row(0), s_wm.at[i])
        left(ga(0, 0), s_zp.at[i])
        left(az_p.at[0], s_ap.at[i])
    for i in range(8):
        left(ga(0, 0), s_xr.at[i])
        left(ga(0, 0), s_xl.at[i])
        left(ga(0, 0), s_xf.at[i])
        left(ga_row(0), s_sd.at[i])
        left(gb_row(0), s_se.at[i])
        left(ax_f.at[0], s_af.at[i])
        left(ax_f.at[0], s_al.at[i])
        left(ax_f.at[0], s_ar.at[i])
    for c in range(4):
        for s in range(4):
            left(b_m.at[0, 0], s_bm.at[c, s])
        for s in range(3):
            left(b_p.at[0, 0], s_bp.at[c, s])
    left(sib.at[:, :, :, sa], s_d2.at[0])
    left(sib.at[:, :, :, sb], s_d2.at[1])


def local(particles, offsets, ref_maps, inv_sigma2, log_prior, orient):
    f32, bf16 = jnp.float32, jnp.bfloat16
    vmem = pl.BlockSpec(memory_space=pltpu.VMEM)
    smem = pl.BlockSpec(memory_space=pltpu.SMEM)
    dma = pltpu.SemaphoreType.DMA

    def twice(*shape):
        return [dma(shape), dma(shape)] if shape else [dma, dma]

    scratch = [
        pltpu.VMEM((16, PACK), f32),
        pltpu.VMEM((16, PACK), bf16),
        pltpu.VMEM((2, ZN, XN, 16, PACK), bf16),
        pltpu.VMEM((2, 2, HALF, FPIX), bf16),
        pltpu.VMEM((2, HALF, 128), jnp.int32),
        pltpu.VMEM((3, HALF, 128), f32),
        pltpu.VMEM((ROWS, WIDTH), bf16),
        pltpu.VMEM((256, WIDTH), bf16),
        pltpu.VMEM((256, ROWS), f32),
        pltpu.VMEM((256, ROWS), bf16),
        pltpu.VMEM((4, 2, 8, 128), f32),
        pltpu.VMEM((32, 2, 8, SUMW), f32),
        pltpu.VMEM((16, 2, 8, SUMW), f32),
        pltpu.VMEM((8, SUMW), f32),
        pltpu.VMEM((2, 8, 128), f32),
        pltpu.VMEM((8, 8, SCUT), f32),
        pltpu.VMEM((8, 8, SCUT), f32),
        pltpu.VMEM((8, 8, SCUT), f32),
        pltpu.VMEM((4, 8, SCUT), f32),
        pltpu.VMEM((3, 8, SCUT), f32),
        pltpu.VMEM((4, 3, 8, SUMW - SCUT), f32),
        pltpu.VMEM((4, 4, 8, SUMW - SCUT), f32),
        pltpu.VMEM((8, SUMW - SCUT), f32),
        pltpu.VMEM((8, SUMW - SCUT), f32),
        pltpu.VMEM((8, SUMW - SCUT), f32),
    ]
    scratch += twice() + twice(2) + twice(3) + twice() + twice()
    scratch += twice(4) + twice(3) + twice(8) * 3 + twice(8)
    scratch += twice(3) + twice(3) + twice(4) + twice(8)
    scratch += twice(2) + twice(8) * 3 + twice(4) + twice(3)
    scratch += twice(4, 3) + twice(4, 4) + twice(3)
    sums, counts, loglik = pl.pallas_call(
        kernel,
        out_shape=(
            jax.ShapeDtypeStruct((8, FPIX), f32),
            jax.ShapeDtypeStruct((8, 128), f32),
            jax.ShapeDtypeStruct((8, 128), f32),
        ),
        in_specs=[smem, smem, vmem, vmem, vmem, vmem, vmem],
        out_specs=(vmem, vmem, vmem),
        scratch_shapes=scratch,
        compiler_params=pltpu.CompilerParams(
            collective_id=0, has_side_effects=True, vmem_limit_bytes=56 * 1024 * 1024
        ),
    )(orient, log_prior, inv_sigma2.reshape(1, FPIX), jnp.asarray(tables()), offsets, particles, ref_maps)
    return (
        sums.reshape(2, 2, 2, FPIX).transpose(1, 2, 0, 3).reshape(2, 2, 1, 2, FPIX),
        counts[0:4, 0].reshape(2, 2, 1),
        jnp.stack([loglik[0, 0:64], loglik[2, 0:64]]),
    )


def solution(mesh):
    return jax.shard_map(
        local,
        mesh=mesh,
        in_specs=(
            P("dom", None, None),
            P("dom", None),
            P("cls", "dom", None, None),
            P(),
            P("cls"),
            P(None, "dom"),
        ),
        out_specs=(P(None, "cls", "dom", None, None), P(None, "cls", "dom"), P(None, "dom")),
        check_vma=False,
    )
```

```python
import math

import jax
import jax.numpy as jnp
import numpy as np
from jax import lax
from jax.experimental import pallas as pl
from jax.experimental.pallas import tpu as pltpu
from jax.sharding import PartitionSpec as P

MESH = pl.DeviceIdType.MESH
BOX = 256
KYW = 128
FPIX = 2048
XN = 4
ZN = 8
HALF = 32
STEPS = 25
ROWS = 1792
LIVE = 1600
WIDTH = 2 * FPIX + 128
PACK = 1152
GCUT = 768
SUMW = 128 + FPIX
SCUT = 1664
DELTA = (0, -1, 1, -2, 2, -3, 3, -4)
XPEER = (1, -1, 2)
ZPEER = (1, -1, 2, -2, 3, -3, 4)
ORDER = (4, -3, 3, -2, 2, -1, 1, 0)


def tables():
    table = np.zeros((17, 8, 128), np.float64)
    for step in (1, 2, 3):
        for kx in range(16):
            turn = 2.0 * math.pi * ((kx * step) % BOX) / BOX
            table[kx, 2 * step - 2] = math.cos(turn)
            table[kx, 2 * step - 1] = math.sin(turn)
        ky = np.arange(KYW) - KYW // 2
        turn = 2.0 * math.pi * ((ky * step) % BOX) / BOX
        table[16, 2 * step - 2] = np.cos(turn)
        table[16, 2 * step - 1] = np.sin(turn)
    return table.astype(np.float32)


def by_offset(offset, row):
    size = jnp.abs(offset)
    cosine = jnp.where(
        size < 0.5, 1.0, jnp.where(size < 1.5, row[0:1], jnp.where(size < 2.5, row[2:3], row[4:5]))
    )
    sine = jnp.where(
        size < 0.5, 0.0, jnp.where(size < 1.5, row[1:2], jnp.where(size < 2.5, row[3:4], row[5:6]))
    )
    return cosine, jnp.where(offset < 0, -sine, sine)


def rotations(real, imag, row):
    result = [None] * 5
    result[2] = (real, imag)
    for step in (1, 2):
        cosine, sine = row[2 * step - 2 : 2 * step - 1], row[2 * step - 1 : 2 * step]
        rc, rs, ic, is_ = real * cosine, real * sine, imag * cosine, imag * sine
        result[2 + step] = (rc + is_, ic - rs)
        result[2 - step] = (rc - is_, ic + rs)
    return result


def kernel(
    orient, prior, offsets, noise, table, particles_hbm, maps_hbm,
    sums_out, counts_out, loglik_out,
    particles, maps, block, gath, pix, offs, base, shifted, weights, logits, post, stats,
    part, sib, llr, ax_l, ax_r, ax_f, ae, ag, be, bg, bx,
    s_in, s_pix, r_pix, s_st, r_st, s_ll, r_ll,
    s_z, r_z, s_x, r_x, s_sd, r_sd, s_y, r_y, s_w, r_w, s_se, r_se,
    s_d2, r_d2, s_al, r_al, s_ar, r_ar, s_af, r_af, s_ae, r_ae, s_ag, r_ag,
    s_be, r_be, s_bg, r_bg, s_bx, r_bx,
):
    dom, cls = lax.axis_index("dom"), lax.axis_index("cls")
    y_hi, x, z = lax.div(dom, 32), lax.rem(lax.div(dom, 8), XN), lax.rem(dom, ZN)
    y_lo, core = lax.div(cls, 2), lax.rem(cls, 2)
    y = y_hi * 2 + y_lo

    def device(yy, cc, xx, zz):
        return ((lax.div(yy, 2) * XN + xx) * ZN + zz, lax.rem(yy, 2) * 2 + cc)

    def xat(d):
        return lax.rem(x + (XN + d), XN)

    def zat(d):
        return lax.rem(z + (ZN + d), ZN)

    def yat(d):
        return lax.rem(y + d, 4)

    x_up, x_down = device(y, core, xat(1), z), device(y, core, xat(-1), z)
    sibling = device(y, 1 - core, x, z)
    mate = device(3 - y, core, x, z)
    x_peers = [device(y, core, xat(d), z) for d in XPEER]
    z_peers = [device(y, core, x, zat(d)) for d in ZPEER]
    y_peers = [device(yat(d), core, x, z) for d in (1, 2, 3)]

    def send(src, dst, ssem, rsem, to):
        copy = pltpu.make_async_remote_copy(
            src_ref=src, dst_ref=dst, send_sem=ssem, recv_sem=rsem, device_id=to, device_id_type=MESH
        )
        copy.start()

    def landed(dst, rsem):
        pltpu.make_async_copy(dst, dst, rsem).wait()

    def left(src, ssem):
        pltpu.make_async_copy(src, src, ssem).wait()

    barrier = pltpu.get_barrier_semaphore()
    peers = x_peers + z_peers + y_peers + [sibling]
    for other in peers:
        pl.semaphore_signal(barrier, inc=1, device_id=other, device_id_type=MESH)
    get_maps = pltpu.make_async_copy(maps_hbm, maps, s_in.at[0])
    get_maps.start()
    get_particles = pltpu.make_async_copy(particles_hbm, particles, s_in.at[1])
    get_particles.start()
    get_maps.wait()

    lane = lax.broadcasted_iota(jnp.int32, (1, 128), 1)
    weight = noise[...]
    for r in range(2):
        for k in range(2):
            picked = maps[k, orient[0, r]].astype(jnp.float32)
            scaled = picked * weight
            energy = 0.5 * jnp.sum(jnp.sum(scaled * picked, axis=0, keepdims=True), axis=1, keepdims=True)
            bias = prior[k] - energy
            high = bias.astype(jnp.bfloat16).astype(jnp.float32)
            rest = bias - high
            middle = rest.astype(jnp.bfloat16).astype(jnp.float32)
            low = rest - middle
            row = 2 * r + k
            for q in range(4):
                block[q * 4 + row : q * 4 + row + 1, 0:1024] = scaled[
                    q // 2 : q // 2 + 1, (q % 2) * 1024 : (q % 2) * 1024 + 1024
                ]
                block[q * 4 + row : q * 4 + row + 1, 1024:PACK] = jnp.where(
                    lane == 0, high, jnp.where(lane == 1, middle, jnp.where(lane == 2, low, 0.0))
                )
    gath[core, z, x] = block[...].astype(jnp.bfloat16)
    get_particles.wait()

    first = pl.multiple_of(core * HALF, HALF)
    mine = pl.ds(first, HALF)

    @pl.loop(0, 16)
    def _(tile):
        lanes = pl.ds(pl.multiple_of(tile * 128, 128), 128)
        both = particles[mine, :, lanes].astype(jnp.float32)
        pix[y_hi, 0, :, lanes] = both[:, 0, :].astype(jnp.bfloat16)
        pix[y_hi, 1, :, lanes] = both[:, 1, :].astype(jnp.bfloat16)

    @pl.loop(0, HALF)
    def _(i):
        offs[y_hi, pl.ds(i, 1), :] = jnp.where(lane == 0, offsets[0, first + i], offsets[1, first + i])

    def prepare(h):
        both = offs[h].astype(jnp.float32)
        base[0] = jnp.broadcast_to(both[:, 0:1], (HALF, 128))
        cosine, sine = by_offset(jnp.broadcast_to(both[:, 1:2], (HALF, 128)), table[16])
        base[1] = cosine
        base[2] = sine

    def shift(h, begin, end):
        @pl.loop(begin, end)
        def _(kx):
            start = pl.multiple_of(kx * 128, 128)
            row = table[kx]
            for g in range(0, HALF, 16):
                real = pix[h, 0, g : g + 16, pl.ds(start, 128)].astype(jnp.float32)
                imag = pix[h, 1, g : g + 16, pl.ds(start, 128)].astype(jnp.float32)
                cx, sx = by_offset(base[0, g : g + 16], row)
                cy, sy = base[1, g : g + 16], base[2, g : g + 16]
                cosine, sine = cx * cy - sx * sy, sx * cy + cx * sy
                real, imag = real * cosine + imag * sine, imag * cosine - real * sine
                for iy, (ry, iy_) in enumerate(rotations(real, imag, table[16])):
                    for ix, (rx, im) in enumerate(rotations(ry, iy_, row)):
                        at = pl.ds(pl.multiple_of((iy * 5 + ix) * 64 + g + h * HALF, 16), 16)
                        shifted[at, pl.ds(start, 128)] = rx.astype(jnp.bfloat16)
                        shifted[at, pl.ds(pl.multiple_of(start + FPIX, 128), 128)] = im.astype(jnp.bfloat16)

    prepare(y_hi)
    shift(y_hi, 0, 16)

    wide = lax.broadcasted_iota(jnp.int32, (LIVE, 128), 1)
    shifted[0:LIVE, 2 * FPIX : WIDTH] = jnp.where(wide < 3, 1.0, 0.0).astype(jnp.bfloat16)
    shifted[LIVE:ROWS, :] = jnp.zeros((ROWS - LIVE, WIDTH), jnp.bfloat16)
    post[:, LIVE + 64 : ROWS] = jnp.zeros((256, ROWS - LIVE - 64), jnp.bfloat16)

    pl.semaphore_wait(barrier, len(peers))

    ca, cb = pl.ds(0, GCUT), pl.ds(GCUT, PACK - GCUT)

    def ga(dz, dx):
        return gath.at[core, zat(dz), xat(dx), :, ca]

    def gb(dz, dx):
        return gath.at[core, zat(dz), xat(dx), :, cb]

    def ga_row(dz, c=None):
        return gath.at[core if c is None else c, zat(dz), :, :, ca]

    def gb_row(dz, c=None):
        return gath.at[core if c is None else c, zat(dz), :, :, cb]

    def xs(j):
        ref = ga(DELTA[j], 0)
        for i in range(3):
            send(ref, ref, s_x.at[j, i], r_x.at[j, i], x_peers[i])

    def from_z(j):
        landed(ga(DELTA[j], 0), r_z.at[j - 1])
        xs(j)

    def row_a(j):
        for i in range(3):
            landed(ga(DELTA[j], -XPEER[i]), r_x.at[j, i])
        send(ga_row(DELTA[j]), ga_row(DELTA[j]), s_sd.at[j], r_sd.at[j], sibling)

    def row_b(j):
        send(gb_row(DELTA[j]), gb_row(DELTA[j]), s_se.at[j], r_se.at[j], sibling)

    def w(i, row, step):
        send(gb_row(row), gb_row(row), s_w.at[i], r_w.at[i], device(y, core, x, zat(step)))

    def from_w(i, row, j):
        landed(gb_row(row), r_w.at[i])
        row_b(j)

    for i in range(3):
        send(gb(0, 0), gb(0, 0), s_y.at[i], r_y.at[i], x_peers[i])
    for i in range(7):
        send(ga(0, 0), ga(0, 0), s_z.at[i], r_z.at[i], z_peers[i])
    xs(0)
    send(offs.at[y_hi], offs.at[y_hi], s_pix.at[1], r_pix.at[1], mate)
    send(pix.at[y_hi], pix.at[y_hi], s_pix.at[0], r_pix.at[0], mate)
    for i in range(3):
        landed(gb(0, -XPEER[i]), r_y.at[i])
    for i, step in enumerate((2, -2, 1, -1)):
        w(i, 0, step)
    row_b(0)
    for j in range(1, 5):
        from_z(j)
    row_a(0)
    for j in range(5, 8):
        from_z(j)
    row_a(1)
    from_w(0, -2, 3)
    w(4, -2, 1)
    w(5, -2, 2)
    from_w(1, 2, 4)
    w(6, 2, -1)
    from_w(2, -1, 1)
    from_w(3, 1, 2)
    row_a(2)
    landed(offs.at[1 - y_hi], r_pix.at[1])
    landed(pix.at[1 - y_hi], r_pix.at[0])
    prepare(1 - y_hi)
    shift(1 - y_hi, 0, 6)
    row_a(3)
    row_a(4)
    shift(1 - y_hi, 6, 12)
    row_a(5)
    row_a(6)
    from_w(4, -3, 5)
    from_w(6, 3, 6)
    shift(1 - y_hi, 12, 16)
    from_w(5, -4, 7)
    row_a(7)
    for j in range(8):
        landed(ga_row(DELTA[j], 1 - core), r_sd.at[j])
        landed(gb_row(DELTA[j], 1 - core), r_se.at[j])

    upper = lax.broadcasted_iota(jnp.int32, (8, 1024), 0) < 4

    @pl.loop(0, 16)
    def _(group):
        gb_, gz = lax.div(group, 8), lax.rem(group, 8)
        rows = pl.ds(pl.multiple_of(group * 16, 16), 16)
        tiles = [gath[gb_, gz, i].astype(jnp.float32) for i in range(4)]
        for t in range(2):
            t0, t1, t2, t3 = [tile[8 * t : 8 * t + 8, 0:1024] for tile in tiles]
            weights[rows, 2048 * t : 2048 * t + 1024] = jnp.concatenate(
                [jnp.where(upper, t0, pltpu.roll(t1, 4, 0)), jnp.where(upper, t2, pltpu.roll(t3, 4, 0))], axis=0
            ).astype(jnp.bfloat16)
            weights[rows, 2048 * t + 1024 : 2048 * t + 2048] = jnp.concatenate(
                [jnp.where(upper, pltpu.roll(t0, 4, 0), t1), jnp.where(upper, pltpu.roll(t2, 4, 0), t3)], axis=0
            ).astype(jnp.bfloat16)
        t0, t1, t2, t3 = [tile[0:8, 1024:PACK] for tile in tiles]
        up = upper[:, 0:128]
        weights[rows, 2 * FPIX : WIDTH] = jnp.concatenate(
            [jnp.where(up, t0, pltpu.roll(t1, 4, 0)), jnp.where(up, t2, pltpu.roll(t3, 4, 0))], axis=0
        ).astype(jnp.bfloat16)

    @pl.loop(0, 2)
    def _(tile):
        at = pl.ds(pl.multiple_of(tile * 896, 128), 896)
        logits[:, at] = lax.dot_general(
            shifted[at, :], weights[...], (((1,), (1,)), ((), ())), preferred_element_type=jnp.float32
        ).T

    sub = lax.broadcasted_iota(jnp.int32, (8, 128), 0)

    def over_group(value, join):
        value = join(value, pltpu.roll(value, 4, 0))
        value = join(value, jnp.where(sub % 2 == 0, pltpu.roll(value, 7, 0), pltpu.roll(value, 1, 0)))
        return join(value, pltpu.roll(value, 64, 1))

    live = lax.broadcasted_iota(jnp.int32, (256, 128), 1) < 64
    last = pl.ds(LIVE - 64, 128)
    logits[:, last] = jnp.where(live, logits[:, last], -3.0e38)

    def peak_of(tile, carry):
        at = pl.ds(pl.multiple_of(tile * 128, 128), 128)
        return jnp.maximum(carry, jnp.max(logits[:, at].reshape(32, 8, 128), axis=0))

    peak = over_group(lax.fori_loop(0, 13, peak_of, jnp.full((8, 128), -3.0e38, jnp.float32)), jnp.maximum)

    def total_of(tile, carry):
        at = pl.ds(pl.multiple_of(tile * 128, 128), 128)
        value = jnp.exp(logits[:, at].reshape(32, 8, 128) - peak[None])
        logits[:, at] = value.reshape(256, 128)
        return carry + jnp.sum(value, axis=0)

    total = over_group(lax.fori_loop(0, 13, total_of, jnp.zeros((8, 128), jnp.float32)), jnp.add)

    stats[y, 0] = peak
    stats[y, 1] = total
    for i in range(3):
        send(stats.at[y], stats.at[y], s_st.at[i], r_st.at[i], y_peers[i])
    for i in range(3):
        landed(stats.at[yat(3 - i)], r_st.at[i])
    peaks = [stats[i, 0] for i in range(4)]
    top = jnp.maximum(jnp.maximum(peaks[0], peaks[1]), jnp.maximum(peaks[2], peaks[3]))
    whole = stats[0, 1] * jnp.exp(peaks[0] - top)
    for i in range(1, 4):
        whole = whole + stats[i, 1] * jnp.exp(peaks[i] - top)
    scale = jnp.exp(peak - top) / whole
    llr[core] = top + jnp.log(whole)
    send(llr.at[core], llr.at[core], s_ll, r_ll, sibling)

    @pl.loop(0, 13)
    def _(tile):
        at = pl.ds(pl.multiple_of(tile * 128, 128), 128)
        value = logits[:, at].reshape(32, 8, 128) * scale[None]
        post[:, at] = value.reshape(256, 128).astype(jnp.bfloat16)

    def product(at):
        return jnp.dot(post[...], shifted[:, at], preferred_element_type=jnp.float32)

    def store(at, top_, bottom, width):
        keep = lax.broadcasted_iota(jnp.int32, (256, width), 0) % 8 < 4
        even = jnp.where(keep, top_, pltpu.roll(bottom, 4, 0))
        odd = jnp.where(keep, pltpu.roll(top_, 252, 0), bottom)
        part[:, 0, :, at] = even.reshape(32, 8, width)
        part[:, 1, :, at] = odd.reshape(32, 8, width)

    def trade(at, i):
        send(part.at[pl.ds((1 - core) * 16, 16), :, :, at], sib.at[:, :, :, at], s_d2.at[i], r_d2.at[i], sibling)

    def collect(at, i):
        landed(sib.at[:, :, :, at], r_d2.at[i])

        @pl.loop(0, 16)
        def _(pair):
            row = core * 16 + pair
            part[row, :, :, at] = part[row, :, :, at] + sib[pair, :, :, at]

    sa, sb = pl.ds(0, SCUT), pl.ds(SCUT, SUMW - SCUT)

    def pa(dz, dx, at):
        xx = xat(dx)
        return part.at[core * 16 + zat(dz) * 2 + lax.div(xx, 2), lax.rem(xx, 2), :, at]

    def add(dst, src):
        dst[...] = dst[...] + src[...]

    def a_away(i):
        to = x_up if i % 2 == 0 else x_down
        send(pa(ORDER[i], 2, sa), ax_f.at[i], s_af.at[i], r_af.at[i], to)

    def a_near(i):
        if i % 2 == 0:
            send(pa(ORDER[i], -1, sa), ax_r.at[i], s_ar.at[i], r_ar.at[i], x_down)
        else:
            send(pa(ORDER[i], 1, sa), ax_l.at[i], s_al.at[i], r_al.at[i], x_up)

    def a_far(i):
        d = ORDER[i]
        landed(ax_f.at[i], r_af.at[i])
        if i % 2 == 0:
            add(ax_f.at[i], pa(d, 1, sa))
            send(ax_f.at[i], ax_l.at[i], s_al.at[i], r_al.at[i], x_up)
        else:
            add(ax_f.at[i], pa(d, -1, sa))
            send(ax_f.at[i], ax_r.at[i], s_ar.at[i], r_ar.at[i], x_down)

    def a_sum(i):
        own_ = pa(ORDER[i], 0, sa)
        landed(ax_l.at[i], r_al.at[i])
        landed(ax_r.at[i], r_ar.at[i])
        own_[...] = own_[...] + ax_l[i] + ax_r[i]
        if i < 3:
            send(own_, ae.at[i], s_ae.at[i], r_ae.at[i], device(y, core, x, zat((-2, -1, 1)[i])))
        elif i in (5, 6):
            send(own_, ag.at[i - 5], s_ag.at[i - 5], r_ag.at[i - 5], device(y, core, x, zat(ORDER[i])))

    def a_join():
        ref = pa(-2, 0, sa)
        landed(ae.at[0], r_ae.at[0])
        landed(ae.at[1], r_ae.at[1])
        ref[...] = ref[...] + ae[0] + ae[1]
        send(ref, ag.at[2], s_ag.at[2], r_ag.at[2], device(y, core, x, zat(-2)))
        ref = pa(2, 0, sa)
        landed(ae.at[2], r_ae.at[2])
        ref[...] = ref[...] + ae[2]
        send(ref, ag.at[3], s_ag.at[3], r_ag.at[3], device(y, core, x, zat(2)))

    def a_end():
        own_ = pa(0, 0, sa)
        for i in range(4):
            landed(ag.at[i], r_ag.at[i])
        own_[...] = own_[...] + ((ag[0] + ag[1]) + (ag[2] + ag[3]))

    def pb(dz):
        return part.at[pl.ds(core * 16 + zat(dz) * 2, 2), :, :, sb]

    def b_start():
        for i, (row, step) in enumerate(((4, 2), (3, 1), (-3, -1))):
            send(pb(row), be.at[i], s_be.at[i], r_be.at[i], device(y, core, x, zat(step)))
        for i, step in enumerate((-1, 1)):
            send(pb(step), bg.at[i], s_bg.at[i], r_bg.at[i], device(y, core, x, zat(step)))

    def b_join():
        landed(be.at[0], r_be.at[0])
        landed(be.at[1], r_be.at[1])
        ref = pb(2)
        ref[...] = ref[...] + be[0] + be[1]
        send(ref, bg.at[2], s_bg.at[2], r_bg.at[2], device(y, core, x, zat(2)))
        landed(be.at[2], r_be.at[2])
        ref = pb(-2)
        ref[...] = ref[...] + be[2]
        send(ref, bg.at[3], s_bg.at[3], r_bg.at[3], device(y, core, x, zat(-2)))

    def b_sum():
        for i in range(4):
            landed(bg.at[i], r_bg.at[i])
        ref = pb(0)
        ref[...] = ref[...] + ((bg[0] + bg[1]) + (bg[2] + bg[3]))
        for i in range(3):
            send(pa(0, XPEER[i], sb), bx.at[i], s_bx.at[i], r_bx.at[i], x_peers[i])

    def b_end():
        own_ = pa(0, 0, sb)
        for i in range(3):
            landed(bx.at[i], r_bx.at[i])
        own_[...] = own_[...] + bx[0] + (bx[1] + bx[2])

    def piece(start, width):
        store(
            pl.ds(128 + start, width), product(pl.ds(start, width)), product(pl.ds(FPIX + start, width)), width
        )

    cuts = [pl.ds(0, 640), pl.ds(640, 512), pl.ds(1152, 512)]
    piece(1536, 512)
    trade(sb, 3)
    edge = product(pl.ds(2 * FPIX, 128))
    store(pl.ds(0, 128), edge, edge, 128)
    piece(0, 512)
    trade(cuts[0], 0)
    piece(512, 512)
    trade(cuts[1], 1)
    collect(sb, 3)
    b_start()
    piece(1024, 512)
    trade(cuts[2], 2)
    for i in range(3):
        collect(cuts[i], i)
    for i in range(6):
        a_away(i)
    a_near(1)
    a_near(0)
    b_join()
    a_far(0)
    a_far(1)
    a_away(6)
    a_away(7)
    a_far(2)
    a_far(3)
    a_near(3)
    a_near(2)
    a_far(4)
    a_far(5)
    a_near(5)
    a_near(4)
    a_sum(0)
    a_sum(1)
    b_sum()
    a_far(6)
    a_far(7)
    a_near(7)
    a_near(6)
    a_sum(2)
    a_sum(3)
    a_sum(4)
    a_join()
    a_sum(5)
    a_sum(6)
    b_end()
    a_sum(7)
    a_end()

    done = part[core * 16 + z * 2 + lax.div(x, 2), lax.rem(x, 2)]
    pair = lax.broadcasted_iota(jnp.int32, (1, 2), 1)
    for r in range(2):
        counts_out[r] = jnp.where(pair == 0, done[2 * r : 2 * r + 1, 0:1], done[2 * r + 1 : 2 * r + 2, 0:1])
        for k in range(2):
            for c in range(2):
                row = 4 * c + 2 * r + k
                sums_out[r, k, c : c + 1, :] = done[row : row + 1, 128:SUMW]

    landed(llr.at[1 - core], r_ll)
    value = jnp.where(
        lax.broadcasted_iota(jnp.int32, (8, 128), 1) < 32,
        jnp.where(y_hi == 0, llr[0], pltpu.roll(llr[0], 96, 1)),
        jnp.where(y_hi == 1, llr[1], pltpu.roll(llr[1], 32, 1)),
    )
    loglik_out[0:1, :] = value[0:1, 0:64]
    loglik_out[1:2, :] = value[2:3, 0:64]

    left(pix.at[0], s_pix.at[0])
    left(offs.at[0], s_pix.at[1])
    left(llr.at[0], s_ll)
    for i in range(3):
        left(stats.at[0], s_st.at[i])
        left(gb(0, 0), s_y.at[i])
        left(be.at[0], s_be.at[i])
        left(ae.at[0], s_ae.at[i])
        left(bx.at[0], s_bx.at[i])
    for i in range(4):
        left(bg.at[0], s_bg.at[i])
        left(ag.at[0], s_ag.at[i])
    for i in range(7):
        left(ga(0, 0), s_z.at[i])
        left(gb_row(0), s_w.at[i])
    for i in range(8):
        for k in range(3):
            left(ga(0, 0), s_x.at[i, k])
        left(ga_row(0), s_sd.at[i])
        left(gb_row(0), s_se.at[i])
        left(ax_f.at[0], s_af.at[i])
        left(ax_f.at[0], s_al.at[i])
        left(ax_f.at[0], s_ar.at[i])
    for i in range(3):
        left(sib.at[:, :, :, cuts[i]], s_d2.at[i])
    left(sib.at[:, :, :, sb], s_d2.at[3])


def local(particles, offsets, ref_maps, inv_sigma2, log_prior, orient):
    f32, bf16 = jnp.float32, jnp.bfloat16
    vmem = pl.BlockSpec(memory_space=pltpu.VMEM)
    smem = pl.BlockSpec(memory_space=pltpu.SMEM)
    dma = pltpu.SemaphoreType.DMA

    def twice(*shape):
        return [dma(shape), dma(shape)] if shape else [dma, dma]

    rest = SUMW - SCUT
    scratch = [
        pltpu.VMEM((64, 2, FPIX), bf16),
        pltpu.VMEM((2, 64, 2, FPIX), bf16),
        pltpu.VMEM((16, PACK), f32),
        pltpu.VMEM((2, ZN, XN, 16, PACK), bf16),
        pltpu.VMEM((2, 2, HALF, FPIX), bf16),
        pltpu.VMEM((2, HALF, 128), jnp.int32),
        pltpu.VMEM((3, HALF, 128), f32),
        pltpu.VMEM((ROWS, WIDTH), bf16),
        pltpu.VMEM((256, WIDTH), bf16),
        pltpu.VMEM((256, ROWS), f32),
        pltpu.VMEM((256, ROWS), bf16),
        pltpu.VMEM((4, 2, 8, 128), f32),
        pltpu.VMEM((32, 2, 8, SUMW), f32),
        pltpu.VMEM((16, 2, 8, SUMW), f32),
        pltpu.VMEM((2, 8, 128), f32),
        pltpu.VMEM((8, 8, SCUT), f32),
        pltpu.VMEM((8, 8, SCUT), f32),
        pltpu.VMEM((8, 8, SCUT), f32),
        pltpu.VMEM((3, 8, SCUT), f32),
        pltpu.VMEM((4, 8, SCUT), f32),
        pltpu.VMEM((3, 2, 2, 8, rest), f32),
        pltpu.VMEM((4, 2, 2, 8, rest), f32),
        pltpu.VMEM((3, 8, rest), f32),
    ]
    scratch += [dma((2,))] + twice(2) + twice(3) + twice()
    scratch += twice(7) + twice(8, 3) + twice(8) + twice(3) + twice(7) + twice(8)
    scratch += twice(4) + twice(8) * 3 + twice(3) + twice(4)
    scratch += twice(3) + twice(4) + twice(3)
    hbm = pl.BlockSpec(memory_space=pl.ANY)
    sums, counts, loglik = pl.pallas_call(
        kernel,
        out_shape=(
            jax.ShapeDtypeStruct((2, 2, 2, FPIX), f32),
            jax.ShapeDtypeStruct((2, 1, 2), f32),
            jax.ShapeDtypeStruct((2, 64), f32),
        ),
        in_specs=[smem, smem, smem, vmem, vmem, hbm, hbm],
        out_specs=(vmem, vmem, vmem),
        scratch_shapes=scratch,
        compiler_params=pltpu.CompilerParams(
            collective_id=0, has_side_effects=True, vmem_limit_bytes=56 * 1024 * 1024
        ),
    )(orient.T, log_prior, offsets.T, inv_sigma2.reshape(1, FPIX), jnp.asarray(tables()), particles, ref_maps)
    return sums.reshape(2, 2, 1, 2, FPIX), counts.transpose(0, 2, 1), loglik


def solution(mesh):
    return jax.shard_map(
        local,
        mesh=mesh,
        in_specs=(
            P("dom", None, None),
            P("dom", None),
            P("cls", "dom", None, None),
            P(),
            P("cls"),
            P(None, "dom"),
        ),
        out_specs=(P(None, "cls", "dom", None, None), P(None, "cls", "dom"), P(None, "dom")),
        check_vma=False,
    )
```

```python
import math

import jax
import jax.numpy as jnp
import numpy as np
from jax import lax
from jax.experimental import pallas as pl
from jax.experimental.pallas import tpu as pltpu
from jax.sharding import PartitionSpec as P

MESH = pl.DeviceIdType.MESH
BOX = 256
KYW = 128
FPIX = 2048
XN = 4
ZN = 8
HALF = 32
STEPS = 25
ROWS = 1792
LIVE = 1600
WIDTH = 2 * FPIX + 128
PACK = 1152
GCUT = 768
SUMW = 128 + FPIX
SCUT = 1664
DELTA = (0, -1, 1, -2, 2, -3, 3, -4)
XPEER = (1, -1, 2)
ZPEER = (1, -1, 2, -2, 3, -3, 4)
ORDER = (4, -3, 3, -2, 2, -1, 1, 0)


def tables():
    table = np.zeros((17, 8, 128), np.float64)
    for step in (1, 2, 3):
        for kx in range(16):
            turn = 2.0 * math.pi * ((kx * step) % BOX) / BOX
            table[kx, 2 * step - 2] = math.cos(turn)
            table[kx, 2 * step - 1] = math.sin(turn)
        ky = np.arange(KYW) - KYW // 2
        turn = 2.0 * math.pi * ((ky * step) % BOX) / BOX
        table[16, 2 * step - 2] = np.cos(turn)
        table[16, 2 * step - 1] = np.sin(turn)
    return table.astype(np.float32)


def by_offset(offset, row):
    size = jnp.abs(offset)
    cosine = jnp.where(
        size < 0.5, 1.0, jnp.where(size < 1.5, row[0:1], jnp.where(size < 2.5, row[2:3], row[4:5]))
    )
    sine = jnp.where(
        size < 0.5, 0.0, jnp.where(size < 1.5, row[1:2], jnp.where(size < 2.5, row[3:4], row[5:6]))
    )
    return cosine, jnp.where(offset < 0, -sine, sine)


def rotations(real, imag, row):
    result = [None] * 5
    result[2] = (real, imag)
    for step in (1, 2):
        cosine, sine = row[2 * step - 2 : 2 * step - 1], row[2 * step - 1 : 2 * step]
        rc, rs, ic, is_ = real * cosine, real * sine, imag * cosine, imag * sine
        result[2 + step] = (rc + is_, ic - rs)
        result[2 - step] = (rc - is_, ic + rs)
    return result


def kernel(
    orient, prior, offsets, noise, table, particles_hbm, maps_hbm,
    sums_out, counts_out, loglik_out,
    particles, maps, block, gath, pix, offs, base, shifted, weights, logits, post, stats,
    part, sib, llr, ax_l, ax_r, ax_f, ae, ag, be, bg, bx,
    s_in, s_pix, r_pix, s_st, r_st, s_ll, r_ll,
    s_z, r_z, s_x, r_x, s_sd, r_sd, s_y, r_y, s_w, r_w, s_se, r_se,
    s_d2, r_d2, s_al, r_al, s_ar, r_ar, s_af, r_af, s_ae, r_ae, s_ag, r_ag,
    s_be, r_be, s_bg, r_bg, s_bx, r_bx,
):
    dom, cls = lax.axis_index("dom"), lax.axis_index("cls")
    y_hi, x, z = lax.div(dom, 32), lax.rem(lax.div(dom, 8), XN), lax.rem(dom, ZN)
    y_lo, core = lax.div(cls, 2), lax.rem(cls, 2)
    y = y_hi * 2 + y_lo

    def device(yy, cc, xx, zz):
        return ((lax.div(yy, 2) * XN + xx) * ZN + zz, lax.rem(yy, 2) * 2 + cc)

    def xat(d):
        return lax.rem(x + (XN + d), XN)

    def zat(d):
        return lax.rem(z + (ZN + d), ZN)

    def yat(d):
        return lax.rem(y + d, 4)

    x_up, x_down = device(y, core, xat(1), z), device(y, core, xat(-1), z)
    sibling = device(y, 1 - core, x, z)
    mate = device(3 - y, core, x, z)
    x_peers = [device(y, core, xat(d), z) for d in XPEER]
    z_peers = [device(y, core, x, zat(d)) for d in ZPEER]
    y_peers = [device(yat(d), core, x, z) for d in (1, 2, 3)]

    def send(src, dst, ssem, rsem, to):
        copy = pltpu.make_async_remote_copy(
            src_ref=src, dst_ref=dst, send_sem=ssem, recv_sem=rsem, device_id=to, device_id_type=MESH
        )
        copy.start()

    def landed(dst, rsem):
        pltpu.make_async_copy(dst, dst, rsem).wait()

    def left(src, ssem):
        pltpu.make_async_copy(src, src, ssem).wait()

    barrier = pltpu.get_barrier_semaphore()
    peers = x_peers + z_peers + y_peers + [sibling]
    for other in peers:
        pl.semaphore_signal(barrier, inc=1, device_id=other, device_id_type=MESH)
    get_maps = pltpu.make_async_copy(maps_hbm, maps, s_in.at[0])
    get_maps.start()
    get_particles = pltpu.make_async_copy(particles_hbm, particles, s_in.at[1])
    get_particles.start()
    get_maps.wait()

    lane = lax.broadcasted_iota(jnp.int32, (1, 128), 1)
    weight = noise[...]
    for r in range(2):
        for k in range(2):
            picked = maps[k, orient[0, r]].astype(jnp.float32)
            scaled = picked * weight
            energy = 0.5 * jnp.sum(jnp.sum(scaled * picked, axis=0, keepdims=True), axis=1, keepdims=True)
            bias = prior[k] - energy
            high = bias.astype(jnp.bfloat16).astype(jnp.float32)
            rest = bias - high
            middle = rest.astype(jnp.bfloat16).astype(jnp.float32)
            low = rest - middle
            row = 2 * r + k
            for q in range(4):
                block[q * 4 + row : q * 4 + row + 1, 0:1024] = scaled[
                    q // 2 : q // 2 + 1, (q % 2) * 1024 : (q % 2) * 1024 + 1024
                ]
                block[q * 4 + row : q * 4 + row + 1, 1024:PACK] = jnp.where(
                    lane == 0, high, jnp.where(lane == 1, middle, jnp.where(lane == 2, low, 0.0))
                )
    gath[core, z, x] = block[...].astype(jnp.bfloat16)
    get_particles.wait()

    first = pl.multiple_of(core * HALF, HALF)
    mine = pl.ds(first, HALF)

    @pl.loop(0, 16)
    def _(tile):
        lanes = pl.ds(pl.multiple_of(tile * 128, 128), 128)
        both = particles[mine, :, lanes].astype(jnp.float32)
        pix[y_hi, 0, :, lanes] = both[:, 0, :].astype(jnp.bfloat16)
        pix[y_hi, 1, :, lanes] = both[:, 1, :].astype(jnp.bfloat16)

    @pl.loop(0, HALF)
    def _(i):
        offs[y_hi, pl.ds(i, 1), :] = jnp.where(lane == 0, offsets[0, first + i], offsets[1, first + i])

    def prepare(h):
        both = offs[h].astype(jnp.float32)
        base[0] = jnp.broadcast_to(both[:, 0:1], (HALF, 128))
        cosine, sine = by_offset(jnp.broadcast_to(both[:, 1:2], (HALF, 128)), table[16])
        base[1] = cosine
        base[2] = sine

    def shift(h, begin, end):
        @pl.loop(begin, end)
        def _(kx):
            start = pl.multiple_of(kx * 128, 128)
            row = table[kx]
            for g in range(0, HALF, 16):
                real = pix[h, 0, g : g + 16, pl.ds(start, 128)].astype(jnp.float32)
                imag = pix[h, 1, g : g + 16, pl.ds(start, 128)].astype(jnp.float32)
                cx, sx = by_offset(base[0, g : g + 16], row)
                cy, sy = base[1, g : g + 16], base[2, g : g + 16]
                cosine, sine = cx * cy - sx * sy, sx * cy + cx * sy
                real, imag = real * cosine + imag * sine, imag * cosine - real * sine
                for iy, (ry, iy_) in enumerate(rotations(real, imag, table[16])):
                    for ix, (rx, im) in enumerate(rotations(ry, iy_, row)):
                        at = pl.ds(pl.multiple_of((iy * 5 + ix) * 64 + g + h * HALF, 16), 16)
                        shifted[at, pl.ds(start, 128)] = rx.astype(jnp.bfloat16)
                        shifted[at, pl.ds(pl.multiple_of(start + FPIX, 128), 128)] = im.astype(jnp.bfloat16)

    prepare(y_hi)
    shift(y_hi, 0, 16)

    wide = lax.broadcasted_iota(jnp.int32, (LIVE, 128), 1)
    shifted[0:LIVE, 2 * FPIX : WIDTH] = jnp.where(wide < 3, 1.0, 0.0).astype(jnp.bfloat16)
    shifted[LIVE:ROWS, :] = jnp.zeros((ROWS - LIVE, WIDTH), jnp.bfloat16)
    post[:, LIVE + 64 : ROWS] = jnp.zeros((256, ROWS - LIVE - 64), jnp.bfloat16)

    pl.semaphore_wait(barrier, len(peers))

    ca, cb = pl.ds(0, GCUT), pl.ds(GCUT, PACK - GCUT)

    def ga(dz, dx):
        return gath.at[core, zat(dz), xat(dx), :, ca]

    def gb(dz, dx):
        return gath.at[core, zat(dz), xat(dx), :, cb]

    def ga_row(dz, c=None):
        return gath.at[core if c is None else c, zat(dz), :, :, ca]

    def gb_row(dz, c=None):
        return gath.at[core if c is None else c, zat(dz), :, :, cb]

    def xs(j):
        ref = ga(DELTA[j], 0)
        for i in range(3):
            send(ref, ref, s_x.at[j, i], r_x.at[j, i], x_peers[i])

    def from_z(j):
        landed(ga(DELTA[j], 0), r_z.at[j - 1])
        xs(j)

    def row_a(j):
        for i in range(3):
            landed(ga(DELTA[j], -XPEER[i]), r_x.at[j, i])
        send(ga_row(DELTA[j]), ga_row(DELTA[j]), s_sd.at[j], r_sd.at[j], sibling)

    def row_b(j):
        send(gb_row(DELTA[j]), gb_row(DELTA[j]), s_se.at[j], r_se.at[j], sibling)

    def w(i, row, step):
        send(gb_row(row), gb_row(row), s_w.at[i], r_w.at[i], device(y, core, x, zat(step)))

    def from_w(i, row, j):
        landed(gb_row(row), r_w.at[i])
        row_b(j)

    for i in range(3):
        send(gb(0, 0), gb(0, 0), s_y.at[i], r_y.at[i], x_peers[i])
    for i in range(7):
        send(ga(0, 0), ga(0, 0), s_z.at[i], r_z.at[i], z_peers[i])
    xs(0)
    send(offs.at[y_hi], offs.at[y_hi], s_pix.at[1], r_pix.at[1], mate)
    send(pix.at[y_hi], pix.at[y_hi], s_pix.at[0], r_pix.at[0], mate)
    for i in range(3):
        landed(gb(0, -XPEER[i]), r_y.at[i])
    for i, step in enumerate((2, -2, 1, -1)):
        w(i, 0, step)
    row_b(0)
    for j in range(1, 5):
        from_z(j)
    row_a(0)
    for j in range(5, 8):
        from_z(j)
    row_a(1)
    from_w(0, -2, 3)
    w(4, -2, 1)
    w(5, -2, 2)
    from_w(1, 2, 4)
    w(6, 2, -1)
    from_w(2, -1, 1)
    from_w(3, 1, 2)
    def spread(c, j, begin, end):
        width = end - begin
        rows = pl.ds(pl.multiple_of((c * 8 + zat(DELTA[j])) * 16, 16), 16)
        upper = lax.broadcasted_iota(jnp.int32, (8, width), 0) < 4
        tiles = [gath[c, zat(DELTA[j]), i, :, begin:end].astype(jnp.float32) for i in range(4)]
        for t in range(2):
            t0, t1, t2, t3 = [tile[8 * t : 8 * t + 8] for tile in tiles]
            place = 2048 * t + begin if begin < 1024 else 2 * FPIX
            weights[rows, place : place + width] = jnp.concatenate(
                [jnp.where(upper, t0, pltpu.roll(t1, 4, 0)), jnp.where(upper, t2, pltpu.roll(t3, 4, 0))], axis=0
            ).astype(jnp.bfloat16)
            if begin == 1024:
                break
            place = 2048 * t + 1024 + begin
            weights[rows, place : place + width] = jnp.concatenate(
                [jnp.where(upper, pltpu.roll(t0, 4, 0), t1), jnp.where(upper, pltpu.roll(t2, 4, 0), t3)], axis=0
            ).astype(jnp.bfloat16)

    def own_a(*which):
        for j in which:
            spread(core, j, 0, GCUT)

    def own_b(*which):
        for j in which:
            spread(core, j, GCUT, 1024)
            spread(core, j, 1024, PACK)

    def sib_a(*which):
        for j in which:
            landed(ga_row(DELTA[j], 1 - core), r_sd.at[j])
            spread(1 - core, j, 0, GCUT)

    def sib_b(*which):
        for j in which:
            landed(gb_row(DELTA[j], 1 - core), r_se.at[j])
            spread(1 - core, j, GCUT, 1024)
            spread(1 - core, j, 1024, PACK)

    row_a(2)
    own_a(0, 1)
    own_b(0)
    sib_a(0)
    sib_b(0)
    landed(offs.at[1 - y_hi], r_pix.at[1])
    landed(pix.at[1 - y_hi], r_pix.at[0])
    prepare(1 - y_hi)
    shift(1 - y_hi, 0, 8)
    row_a(3)
    row_a(4)
    own_a(2)
    own_b(1, 2, 3, 4)
    shift(1 - y_hi, 8, 16)
    row_a(5)
    row_a(6)
    own_a(3, 4)
    sib_a(1, 2)
    sib_b(1, 2, 3, 4)
    from_w(4, -3, 5)
    from_w(6, 3, 6)
    own_a(5, 6)
    own_b(5, 6)
    sib_a(3, 4)
    from_w(5, -4, 7)
    row_a(7)
    own_a(7)
    own_b(7)
    sib_a(5, 6)
    sib_b(5, 6)
    sib_a(7)
    sib_b(7)

    @pl.loop(0, 2)
    def _(tile):
        at = pl.ds(pl.multiple_of(tile * 896, 128), 896)
        logits[:, at] = lax.dot_general(
            shifted[at, :], weights[...], (((1,), (1,)), ((), ())), preferred_element_type=jnp.float32
        ).T

    sub = lax.broadcasted_iota(jnp.int32, (8, 128), 0)

    def over_group(value, join):
        value = join(value, pltpu.roll(value, 4, 0))
        value = join(value, jnp.where(sub % 2 == 0, pltpu.roll(value, 7, 0), pltpu.roll(value, 1, 0)))
        return join(value, pltpu.roll(value, 64, 1))

    live = lax.broadcasted_iota(jnp.int32, (256, 128), 1) < 64
    last = pl.ds(LIVE - 64, 128)
    logits[:, last] = jnp.where(live, logits[:, last], -3.0e38)

    def peak_of(tile, carry):
        at = pl.ds(pl.multiple_of(tile * 128, 128), 128)
        return jnp.maximum(carry, jnp.max(logits[:, at].reshape(32, 8, 128), axis=0))

    peak = over_group(lax.fori_loop(0, 13, peak_of, jnp.full((8, 128), -3.0e38, jnp.float32)), jnp.maximum)

    def total_of(tile, carry):
        at = pl.ds(pl.multiple_of(tile * 128, 128), 128)
        value = jnp.exp(logits[:, at].reshape(32, 8, 128) - peak[None])
        logits[:, at] = value.reshape(256, 128)
        return carry + jnp.sum(value, axis=0)

    total = over_group(lax.fori_loop(0, 13, total_of, jnp.zeros((8, 128), jnp.float32)), jnp.add)

    stats[y, 0] = peak
    stats[y, 1] = total
    for i in range(3):
        send(stats.at[y], stats.at[y], s_st.at[i], r_st.at[i], y_peers[i])
    for i in range(3):
        landed(stats.at[yat(3 - i)], r_st.at[i])
    peaks = [stats[i, 0] for i in range(4)]
    top = jnp.maximum(jnp.maximum(peaks[0], peaks[1]), jnp.maximum(peaks[2], peaks[3]))
    whole = stats[0, 1] * jnp.exp(peaks[0] - top)
    for i in range(1, 4):
        whole = whole + stats[i, 1] * jnp.exp(peaks[i] - top)
    scale = jnp.exp(peak - top) / whole
    llr[core] = top + jnp.log(whole)
    send(llr.at[core], llr.at[core], s_ll, r_ll, sibling)

    @pl.loop(0, 13)
    def _(tile):
        at = pl.ds(pl.multiple_of(tile * 128, 128), 128)
        value = logits[:, at].reshape(32, 8, 128) * scale[None]
        post[:, at] = value.reshape(256, 128).astype(jnp.bfloat16)

    def product(at):
        return jnp.dot(post[...], shifted[:, at], preferred_element_type=jnp.float32)

    def store(at, top_, bottom, width):
        keep = lax.broadcasted_iota(jnp.int32, (256, width), 0) % 8 < 4
        even = jnp.where(keep, top_, pltpu.roll(bottom, 4, 0))
        odd = jnp.where(keep, pltpu.roll(top_, 252, 0), bottom)
        part[:, 0, :, at] = even.reshape(32, 8, width)
        part[:, 1, :, at] = odd.reshape(32, 8, width)

    def trade(at, i):
        send(part.at[pl.ds((1 - core) * 16, 16), :, :, at], sib.at[:, :, :, at], s_d2.at[i], r_d2.at[i], sibling)

    def collect(at, i):
        landed(sib.at[:, :, :, at], r_d2.at[i])

        @pl.loop(0, 16)
        def _(pair):
            row = core * 16 + pair
            part[row, :, :, at] = part[row, :, :, at] + sib[pair, :, :, at]

    sa, sb = pl.ds(0, SCUT), pl.ds(SCUT, SUMW - SCUT)

    def pa(dz, dx, at):
        xx = xat(dx)
        return part.at[core * 16 + zat(dz) * 2 + lax.div(xx, 2), lax.rem(xx, 2), :, at]

    def add(dst, src):
        dst[...] = dst[...] + src[...]

    acols = [pl.ds(0, 896), pl.ds(896, 768)]
    acut = [pl.ds(0, 896), pl.ds(0, 768)]

    def a_away(p, i):
        to = x_up if i % 2 == 0 else x_down
        send(pa(ORDER[i], 2, acols[p]), ax_f.at[p, i, :, acut[p]], s_af.at[p, i], r_af.at[p, i], to)

    def a_near(p, i):
        if i % 2 == 0:
            send(pa(ORDER[i], -1, acols[p]), ax_r.at[p, i, :, acut[p]], s_ar.at[p, i], r_ar.at[p, i], x_down)
        else:
            send(pa(ORDER[i], 1, acols[p]), ax_l.at[p, i, :, acut[p]], s_al.at[p, i], r_al.at[p, i], x_up)

    def a_far(p, i):
        d = ORDER[i]
        landed(ax_f.at[p, i, :, acut[p]], r_af.at[p, i])
        if i % 2 == 0:
            add(ax_f.at[p, i, :, acut[p]], pa(d, 1, acols[p]))
            send(ax_f.at[p, i, :, acut[p]], ax_l.at[p, i, :, acut[p]], s_al.at[p, i], r_al.at[p, i], x_up)
        else:
            add(ax_f.at[p, i, :, acut[p]], pa(d, -1, acols[p]))
            send(ax_f.at[p, i, :, acut[p]], ax_r.at[p, i, :, acut[p]], s_ar.at[p, i], r_ar.at[p, i], x_down)

    def a_sum(p, i):
        own_ = pa(ORDER[i], 0, acols[p])
        landed(ax_l.at[p, i, :, acut[p]], r_al.at[p, i])
        landed(ax_r.at[p, i, :, acut[p]], r_ar.at[p, i])
        own_[...] = own_[...] + ax_l[p, i, :, acut[p]] + ax_r[p, i, :, acut[p]]
        if p == 1 and i in (0, 1, 2):
            send(own_, ae.at[p, i, :, acut[p]], s_ae.at[p, i], r_ae.at[p, i], device(y, core, x, zat(ORDER[i])))
        elif p == 1 and i in (3, 4):
            k = i - 1
            send(own_, ag.at[p, k, :, acut[p]], s_ag.at[p, k], r_ag.at[p, k], device(y, core, x, zat(ORDER[i])))
        elif i < 3:
            send(own_, ae.at[p, i, :, acut[p]], s_ae.at[p, i], r_ae.at[p, i], device(y, core, x, zat((-2, -1, 1)[i])))
        elif i in (5, 6):
            send(own_, ag.at[p, i - 5, :, acut[p]], s_ag.at[p, i - 5], r_ag.at[p, i - 5], device(y, core, x, zat(ORDER[i])))

    def a_join(p):
        ref = pa(-2, 0, acols[p])
        landed(ae.at[p, 0, :, acut[p]], r_ae.at[p, 0])
        landed(ae.at[p, 1, :, acut[p]], r_ae.at[p, 1])
        ref[...] = ref[...] + ae[p, 0, :, acut[p]] + ae[p, 1, :, acut[p]]
        send(ref, ag.at[p, 2, :, acut[p]], s_ag.at[p, 2], r_ag.at[p, 2], device(y, core, x, zat(-2)))
        ref = pa(2, 0, acols[p])
        landed(ae.at[p, 2, :, acut[p]], r_ae.at[p, 2])
        ref[...] = ref[...] + ae[p, 2, :, acut[p]]
        send(ref, ag.at[p, 3, :, acut[p]], s_ag.at[p, 3], r_ag.at[p, 3], device(y, core, x, zat(2)))

    def a_end(p):
        own_ = pa(0, 0, acols[p])
        if p == 1:
            for i in range(3):
                landed(ae.at[p, i, :, acut[p]], r_ae.at[p, i])
            own_[...] = own_[...] + ae[p, 0, :, acut[p]] + (ae[p, 1, :, acut[p]] + ae[p, 2, :, acut[p]])
        for i in range(4):
            landed(ag.at[p, i, :, acut[p]], r_ag.at[p, i])
        own_[...] = own_[...] + ((ag[p, 0, :, acut[p]] + ag[p, 1, :, acut[p]]) + (ag[p, 2, :, acut[p]] + ag[p, 3, :, acut[p]]))

    def pb(dz):
        return part.at[pl.ds(core * 16 + zat(dz) * 2, 2), :, :, sb]

    def b_start():
        for i, (row, step) in enumerate(((4, 2), (3, 1), (-3, -1))):
            send(pb(row), be.at[i], s_be.at[i], r_be.at[i], device(y, core, x, zat(step)))
        for i, step in enumerate((-1, 1)):
            send(pb(step), bg.at[i], s_bg.at[i], r_bg.at[i], device(y, core, x, zat(step)))

    def b_join():
        landed(be.at[0], r_be.at[0])
        landed(be.at[1], r_be.at[1])
        ref = pb(2)
        ref[...] = ref[...] + be[0] + be[1]
        send(ref, bg.at[2], s_bg.at[2], r_bg.at[2], device(y, core, x, zat(2)))
        landed(be.at[2], r_be.at[2])
        ref = pb(-2)
        ref[...] = ref[...] + be[2]
        send(ref, bg.at[3], s_bg.at[3], r_bg.at[3], device(y, core, x, zat(-2)))

    def b_sum():
        for i in range(4):
            landed(bg.at[i], r_bg.at[i])
        ref = pb(0)
        ref[...] = ref[...] + ((bg[0] + bg[1]) + (bg[2] + bg[3]))
        for i in range(3):
            send(pa(0, XPEER[i], sb), bx.at[i], s_bx.at[i], r_bx.at[i], x_peers[i])

    def b_end():
        own_ = pa(0, 0, sb)
        for i in range(3):
            landed(bx.at[i], r_bx.at[i])
        own_[...] = own_[...] + bx[0] + (bx[1] + bx[2])

    def piece(start, width):
        store(
            pl.ds(128 + start, width), product(pl.ds(start, width)), product(pl.ds(FPIX + start, width)), width
        )

    edge = product(pl.ds(2 * FPIX, 128))
    store(pl.ds(0, 128), edge, edge, 128)
    piece(0, 512)
    piece(512, 256)
    trade(acols[0], 0)
    piece(1536, 512)
    trade(sb, 2)
    collect(acols[0], 0)
    for i in range(8):
        a_away(0, i)
    for i in (1, 0, 3, 2):
        a_near(0, i)
    piece(768, 512)
    collect(sb, 2)
    b_start()
    a_far(0, 0)
    a_far(0, 1)
    piece(1280, 256)
    trade(acols[1], 1)
    a_far(0, 2)
    a_far(0, 3)
    a_near(0, 5)
    a_near(0, 4)
    a_far(0, 4)
    a_far(0, 5)
    a_near(0, 7)
    a_near(0, 6)
    a_far(0, 6)
    a_far(0, 7)
    collect(acols[1], 1)
    for i in range(8):
        a_away(1, i)
    for i in (1, 0, 3, 2):
        a_near(1, i)
    for i in range(3):
        a_sum(0, i)
    b_join()
    a_far(1, 0)
    a_far(1, 1)
    a_sum(0, 3)
    a_sum(0, 4)
    a_far(1, 2)
    a_far(1, 3)
    a_near(1, 5)
    a_near(1, 4)
    a_far(1, 4)
    a_far(1, 5)
    a_near(1, 7)
    a_near(1, 6)
    a_sum(0, 5)
    a_sum(0, 6)
    a_join(0)
    a_far(1, 6)
    a_far(1, 7)
    b_sum()
    for i in range(5):
        a_sum(1, i)
    for i in range(5, 8):
        a_sum(1, i)
    a_sum(0, 7)
    b_end()
    a_end(0)
    a_end(1)

    done = part[core * 16 + z * 2 + lax.div(x, 2), lax.rem(x, 2)]
    pair = lax.broadcasted_iota(jnp.int32, (1, 2), 1)
    for r in range(2):
        counts_out[r] = jnp.where(pair == 0, done[2 * r : 2 * r + 1, 0:1], done[2 * r + 1 : 2 * r + 2, 0:1])
        for k in range(2):
            for c in range(2):
                row = 4 * c + 2 * r + k
                sums_out[r, k, c : c + 1, :] = done[row : row + 1, 128:SUMW]

    landed(llr.at[1 - core], r_ll)
    value = jnp.where(
        lax.broadcasted_iota(jnp.int32, (8, 128), 1) < 32,
        jnp.where(y_hi == 0, llr[0], pltpu.roll(llr[0], 96, 1)),
        jnp.where(y_hi == 1, llr[1], pltpu.roll(llr[1], 32, 1)),
    )
    loglik_out[0:1, :] = value[0:1, 0:64]
    loglik_out[1:2, :] = value[2:3, 0:64]

    left(pix.at[0], s_pix.at[0])
    left(offs.at[0], s_pix.at[1])
    left(llr.at[0], s_ll)
    for i in range(3):
        left(stats.at[0], s_st.at[i])
        left(gb(0, 0), s_y.at[i])
        left(be.at[0], s_be.at[i])
        left(bx.at[0], s_bx.at[i])
    for i in range(4):
        left(bg.at[0], s_bg.at[i])
    for i in range(7):
        left(ga(0, 0), s_z.at[i])
        left(gb_row(0), s_w.at[i])
    for i in range(8):
        for k in range(3):
            left(ga(0, 0), s_x.at[i, k])
        left(ga_row(0), s_sd.at[i])
        left(gb_row(0), s_se.at[i])
    for p in range(2):
        for i in range(8):
            left(ax_f.at[p, 0, :, acut[p]], s_af.at[p, i])
            left(ax_f.at[p, 0, :, acut[p]], s_al.at[p, i])
            left(ax_f.at[p, 0, :, acut[p]], s_ar.at[p, i])
        for i in range(3):
            left(ae.at[p, 0, :, acut[p]], s_ae.at[p, i])
        for i in range(4):
            left(ag.at[p, 0, :, acut[p]], s_ag.at[p, i])
        left(sib.at[:, :, :, acols[p]], s_d2.at[p])
    left(sib.at[:, :, :, sb], s_d2.at[2])


def local(particles, offsets, ref_maps, inv_sigma2, log_prior, orient):
    f32, bf16 = jnp.float32, jnp.bfloat16
    vmem = pl.BlockSpec(memory_space=pltpu.VMEM)
    smem = pl.BlockSpec(memory_space=pltpu.SMEM)
    dma = pltpu.SemaphoreType.DMA

    def twice(*shape):
        return [dma(shape), dma(shape)] if shape else [dma, dma]

    rest = SUMW - SCUT
    scratch = [
        pltpu.VMEM((64, 2, FPIX), bf16),
        pltpu.VMEM((2, 64, 2, FPIX), bf16),
        pltpu.VMEM((16, PACK), f32),
        pltpu.VMEM((2, ZN, XN, 16, PACK), bf16),
        pltpu.VMEM((2, 2, HALF, FPIX), bf16),
        pltpu.VMEM((2, HALF, 128), jnp.int32),
        pltpu.VMEM((3, HALF, 128), f32),
        pltpu.VMEM((ROWS, WIDTH), bf16),
        pltpu.VMEM((256, WIDTH), bf16),
        pltpu.VMEM((256, ROWS), f32),
        pltpu.VMEM((256, ROWS), bf16),
        pltpu.VMEM((4, 2, 8, 128), f32),
        pltpu.VMEM((32, 2, 8, SUMW), f32),
        pltpu.VMEM((16, 2, 8, SUMW), f32),
        pltpu.VMEM((2, 8, 128), f32),
        pltpu.VMEM((2, 8, 8, 896), f32),
        pltpu.VMEM((2, 8, 8, 896), f32),
        pltpu.VMEM((2, 8, 8, 896), f32),
        pltpu.VMEM((2, 3, 8, 896), f32),
        pltpu.VMEM((2, 4, 8, 896), f32),
        pltpu.VMEM((3, 2, 2, 8, rest), f32),
        pltpu.VMEM((4, 2, 2, 8, rest), f32),
        pltpu.VMEM((3, 8, rest), f32),
    ]
    scratch += [dma((2,))] + twice(2) + twice(3) + twice()
    scratch += twice(7) + twice(8, 3) + twice(8) + twice(3) + twice(7) + twice(8)
    scratch += twice(3) + twice(2, 8) * 3 + twice(2, 3) + twice(2, 4)
    scratch += twice(3) + twice(4) + twice(3)
    hbm = pl.BlockSpec(memory_space=pl.ANY)
    sums, counts, loglik = pl.pallas_call(
        kernel,
        out_shape=(
            jax.ShapeDtypeStruct((2, 2, 2, FPIX), f32),
            jax.ShapeDtypeStruct((2, 1, 2), f32),
            jax.ShapeDtypeStruct((2, 64), f32),
        ),
        in_specs=[smem, smem, smem, vmem, vmem, hbm, hbm],
        out_specs=(vmem, vmem, vmem),
        scratch_shapes=scratch,
        compiler_params=pltpu.CompilerParams(
            collective_id=0, has_side_effects=True, vmem_limit_bytes=56 * 1024 * 1024
        ),
    )(orient.T, log_prior, offsets.T, inv_sigma2.reshape(1, FPIX), jnp.asarray(tables()), particles, ref_maps)
    return sums.reshape(2, 2, 1, 2, FPIX), counts.transpose(0, 2, 1), loglik


def solution(mesh):
    return jax.shard_map(
        local,
        mesh=mesh,
        in_specs=(
            P("dom", None, None),
            P("dom", None),
            P("cls", "dom", None, None),
            P(),
            P("cls"),
            P(None, "dom"),
        ),
        out_specs=(P(None, "cls", "dom", None, None), P(None, "cls", "dom"), P(None, "dom")),
        check_vma=False,
    )
```

```python
import math

import jax
import jax.numpy as jnp
import numpy as np
from jax import lax
from jax.experimental import pallas as pl
from jax.experimental.pallas import tpu as pltpu
from jax.sharding import PartitionSpec as P

MESH = pl.DeviceIdType.MESH
BOX = 256
KYW = 128
FPIX = 2048
XN = 4
ZN = 8
HALF = 32
STEPS = 25
ROWS = 1792
LIVE = 1600
WIDTH = 2 * FPIX + 128
PACK = 1152
GCUT = 768
SUMW = 128 + FPIX
SCUT = 1664
DELTA = (0, -1, 1, -2, 2, -3, 3, -4)
XPEER = (1, -1, 2)
YPEER = (2, 1, 3)
ZPEER = (1, -1, 2, -2, 3, -3, 4)
ORDER = (4, -3, 3, -2, 2, -1, 1, 0)


def tables():
    table = np.zeros((17, 8, 128), np.float64)
    for step in (1, 2, 3):
        for kx in range(16):
            turn = 2.0 * math.pi * ((kx * step) % BOX) / BOX
            table[kx, 2 * step - 2] = math.cos(turn)
            table[kx, 2 * step - 1] = math.sin(turn)
        ky = np.arange(KYW) - KYW // 2
        turn = 2.0 * math.pi * ((ky * step) % BOX) / BOX
        table[16, 2 * step - 2] = np.cos(turn)
        table[16, 2 * step - 1] = np.sin(turn)
    return table.astype(np.float32)


def by_offset(offset, row):
    size = jnp.abs(offset)
    cosine = jnp.where(
        size < 0.5, 1.0, jnp.where(size < 1.5, row[0:1], jnp.where(size < 2.5, row[2:3], row[4:5]))
    )
    sine = jnp.where(
        size < 0.5, 0.0, jnp.where(size < 1.5, row[1:2], jnp.where(size < 2.5, row[3:4], row[5:6]))
    )
    return cosine, jnp.where(offset < 0, -sine, sine)


def rotations(real, imag, row):
    result = [None] * 5
    result[2] = (real, imag)
    for step in (1, 2):
        cosine, sine = row[2 * step - 2 : 2 * step - 1], row[2 * step - 1 : 2 * step]
        rc, rs, ic, is_ = real * cosine, real * sine, imag * cosine, imag * sine
        result[2 + step] = (rc + is_, ic - rs)
        result[2 - step] = (rc - is_, ic + rs)
    return result


def kernel(
    orient, prior, offsets, noise, table, particles_hbm, maps_hbm,
    sums_out, rest_out,
    particles, maps, block, gath, pix, offs, base, shifted, weights, logits, post, stats,
    part, sib, llr, ax_l, ax_r, ax_f, ae, ag, be, bg, bx,
    s_in, s_pix, r_pix, s_st, r_st, s_ll, r_ll,
    s_z, r_z, s_x, r_x, s_sd, r_sd, s_y, r_y, s_w, r_w, s_se, r_se,
    s_d2, r_d2, s_al, r_al, s_ar, r_ar, s_af, r_af, s_ae, r_ae, s_ag, r_ag,
    s_be, r_be, s_bg, r_bg, s_bx, r_bx,
):
    dom, cls = lax.axis_index("dom"), lax.axis_index("cls")
    y_hi, x, z = lax.div(dom, 32), lax.rem(lax.div(dom, 8), XN), lax.rem(dom, ZN)
    y_lo, core = lax.div(cls, 2), lax.rem(cls, 2)
    y = y_hi * 2 + y_lo

    def device(yy, cc, xx, zz):
        return ((lax.div(yy, 2) * XN + xx) * ZN + zz, lax.rem(yy, 2) * 2 + cc)

    def xat(d):
        return lax.rem(x + (XN + d), XN)

    def zat(d):
        return lax.rem(z + (ZN + d), ZN)

    def yat(d):
        return lax.rem(y + d, 4)

    x_up, x_down = device(y, core, xat(1), z), device(y, core, xat(-1), z)
    sibling = device(y, 1 - core, x, z)
    mate = device(3 - y, core, x, z)
    x_peers = [device(y, core, xat(d), z) for d in XPEER]
    z_peers = [device(y, core, x, zat(d)) for d in ZPEER]
    y_peers = [device(yat(d), core, x, z) for d in YPEER]

    def send(src, dst, ssem, rsem, to):
        copy = pltpu.make_async_remote_copy(
            src_ref=src, dst_ref=dst, send_sem=ssem, recv_sem=rsem, device_id=to, device_id_type=MESH
        )
        copy.start()

    def landed(dst, rsem):
        pltpu.make_async_copy(dst, dst, rsem).wait()

    def left(src, ssem):
        pltpu.make_async_copy(src, src, ssem).wait()

    barrier = pltpu.get_barrier_semaphore()
    peers = x_peers + z_peers + y_peers + [sibling]
    for other in peers:
        pl.semaphore_signal(barrier, inc=1, device_id=other, device_id_type=MESH)
    get_maps = pltpu.make_async_copy(maps_hbm, maps, s_in.at[0])
    get_maps.start()
    get_particles = pltpu.make_async_copy(particles_hbm, particles, s_in.at[1])
    get_particles.start()
    get_maps.wait()

    lane = lax.broadcasted_iota(jnp.int32, (1, 128), 1)
    weight = noise[...]
    for r in range(2):
        for k in range(2):
            picked = maps[k, orient[0, r]].astype(jnp.float32)
            scaled = picked * weight
            energy = 0.5 * jnp.sum(jnp.sum(scaled * picked, axis=0, keepdims=True), axis=1, keepdims=True)
            bias = prior[k] - energy
            high = bias.astype(jnp.bfloat16).astype(jnp.float32)
            rest = bias - high
            middle = rest.astype(jnp.bfloat16).astype(jnp.float32)
            low = rest - middle
            row = 2 * r + k
            for q in range(4):
                block[q * 4 + row : q * 4 + row + 1, 0:1024] = scaled[
                    q // 2 : q // 2 + 1, (q % 2) * 1024 : (q % 2) * 1024 + 1024
                ]
                block[q * 4 + row : q * 4 + row + 1, 1024:PACK] = jnp.where(
                    lane == 0, high, jnp.where(lane == 1, middle, jnp.where(lane == 2, low, 0.0))
                )
    gath[core, z, x] = block[...].astype(jnp.bfloat16)
    get_particles.wait()

    first = pl.multiple_of(core * HALF, HALF)
    mine = pl.ds(first, HALF)

    @pl.loop(0, 16)
    def _(tile):
        lanes = pl.ds(pl.multiple_of(tile * 128, 128), 128)
        both = particles[mine, :, lanes].astype(jnp.float32)
        pix[y_hi, 0, :, lanes] = both[:, 0, :].astype(jnp.bfloat16)
        pix[y_hi, 1, :, lanes] = both[:, 1, :].astype(jnp.bfloat16)

    @pl.loop(0, HALF)
    def _(i):
        offs[y_hi, pl.ds(i, 1), :] = jnp.where(lane == 0, offsets[0, first + i], offsets[1, first + i])

    def prepare(h):
        both = offs[h].astype(jnp.float32)
        base[0] = jnp.broadcast_to(both[:, 0:1], (HALF, 128))
        cosine, sine = by_offset(jnp.broadcast_to(both[:, 1:2], (HALF, 128)), table[16])
        base[1] = cosine
        base[2] = sine

    def shift(h, begin, end):
        @pl.loop(begin, end)
        def _(kx):
            start = pl.multiple_of(kx * 128, 128)
            row = table[kx]
            for g in range(0, HALF, 16):
                real = pix[h, 0, g : g + 16, pl.ds(start, 128)].astype(jnp.float32)
                imag = pix[h, 1, g : g + 16, pl.ds(start, 128)].astype(jnp.float32)
                cx, sx = by_offset(base[0, g : g + 16], row)
                cy, sy = base[1, g : g + 16], base[2, g : g + 16]
                cosine, sine = cx * cy - sx * sy, sx * cy + cx * sy
                real, imag = real * cosine + imag * sine, imag * cosine - real * sine
                for iy, (ry, iy_) in enumerate(rotations(real, imag, table[16])):
                    for ix, (rx, im) in enumerate(rotations(ry, iy_, row)):
                        at = pl.ds(pl.multiple_of((iy * 5 + ix) * 64 + g + h * HALF, 16), 16)
                        shifted[at, pl.ds(start, 128)] = rx.astype(jnp.bfloat16)
                        shifted[at, pl.ds(pl.multiple_of(start + FPIX, 128), 128)] = im.astype(jnp.bfloat16)

    prepare(y_hi)
    shift(y_hi, 0, 16)

    wide = lax.broadcasted_iota(jnp.int32, (LIVE, 128), 1)
    shifted[0:LIVE, 2 * FPIX : WIDTH] = jnp.where(wide < 3, 1.0, 0.0).astype(jnp.bfloat16)
    shifted[LIVE:ROWS, :] = jnp.zeros((ROWS - LIVE, WIDTH), jnp.bfloat16)
    post[:, LIVE + 64 : ROWS] = jnp.zeros((256, ROWS - LIVE - 64), jnp.bfloat16)

    pl.semaphore_wait(barrier, len(peers))

    ca, cb = pl.ds(0, GCUT), pl.ds(GCUT, PACK - GCUT)

    def ga(dz, dx):
        return gath.at[core, zat(dz), xat(dx), :, ca]

    def gb(dz, dx):
        return gath.at[core, zat(dz), xat(dx), :, cb]

    def ga_row(dz, c=None):
        return gath.at[core if c is None else c, zat(dz), :, :, ca]

    def gb_row(dz, c=None):
        return gath.at[core if c is None else c, zat(dz), :, :, cb]

    def xs(j):
        ref = ga(DELTA[j], 0)
        for i in range(3):
            send(ref, ref, s_x.at[j, i], r_x.at[j, i], x_peers[i])

    def from_z(j):
        landed(ga(DELTA[j], 0), r_z.at[j - 1])
        xs(j)

    def row_a(j):
        for i in range(3):
            landed(ga(DELTA[j], -XPEER[i]), r_x.at[j, i])
        send(ga_row(DELTA[j]), ga_row(DELTA[j]), s_sd.at[j], r_sd.at[j], sibling)

    def row_b(j):
        send(gb_row(DELTA[j]), gb_row(DELTA[j]), s_se.at[j], r_se.at[j], sibling)

    def w(i, row, step):
        send(gb_row(row), gb_row(row), s_w.at[i], r_w.at[i], device(y, core, x, zat(step)))

    def from_w(i, row, j):
        landed(gb_row(row), r_w.at[i])
        row_b(j)

    for i in range(3):
        send(gb(0, 0), gb(0, 0), s_y.at[i], r_y.at[i], x_peers[i])
    for i in range(7):
        send(ga(0, 0), ga(0, 0), s_z.at[i], r_z.at[i], z_peers[i])
    xs(0)
    send(offs.at[y_hi], offs.at[y_hi], s_pix.at[1], r_pix.at[1], mate)
    send(pix.at[y_hi], pix.at[y_hi], s_pix.at[0], r_pix.at[0], mate)
    for i in range(3):
        landed(gb(0, -XPEER[i]), r_y.at[i])
    for i, step in enumerate((2, -2, 1, -1)):
        w(i, 0, step)
    row_b(0)
    for j in range(1, 5):
        from_z(j)
    row_a(0)
    for j in range(5, 8):
        from_z(j)
    row_a(1)
    from_w(0, -2, 3)
    w(4, -2, 1)
    w(5, -2, 2)
    from_w(1, 2, 4)
    w(6, 2, -1)
    from_w(2, -1, 1)
    from_w(3, 1, 2)
    def spread(c, j, begin, end):
        width = end - begin
        rows = pl.ds(pl.multiple_of((c * 8 + zat(DELTA[j])) * 16, 16), 16)
        upper = lax.broadcasted_iota(jnp.int32, (8, width), 0) < 4
        tiles = [gath[c, zat(DELTA[j]), i, :, begin:end].astype(jnp.float32) for i in range(4)]
        for t in range(2):
            t0, t1, t2, t3 = [tile[8 * t : 8 * t + 8] for tile in tiles]
            place = 2048 * t + begin if begin < 1024 else 2 * FPIX
            weights[rows, place : place + width] = jnp.concatenate(
                [jnp.where(upper, t0, pltpu.roll(t1, 4, 0)), jnp.where(upper, t2, pltpu.roll(t3, 4, 0))], axis=0
            ).astype(jnp.bfloat16)
            if begin == 1024:
                break
            place = 2048 * t + 1024 + begin
            weights[rows, place : place + width] = jnp.concatenate(
                [jnp.where(upper, pltpu.roll(t0, 4, 0), t1), jnp.where(upper, pltpu.roll(t2, 4, 0), t3)], axis=0
            ).astype(jnp.bfloat16)

    def own_a(*which):
        for j in which:
            spread(core, j, 0, GCUT)

    def own_b(*which):
        for j in which:
            spread(core, j, GCUT, 1024)
            spread(core, j, 1024, PACK)

    def sib_a(*which):
        for j in which:
            landed(ga_row(DELTA[j], 1 - core), r_sd.at[j])
            spread(1 - core, j, 0, GCUT)

    def sib_b(*which):
        for j in which:
            landed(gb_row(DELTA[j], 1 - core), r_se.at[j])
            spread(1 - core, j, GCUT, 1024)
            spread(1 - core, j, 1024, PACK)

    row_a(2)
    own_a(0, 1)
    own_b(0)
    sib_a(0)
    sib_b(0)
    landed(offs.at[1 - y_hi], r_pix.at[1])
    landed(pix.at[1 - y_hi], r_pix.at[0])
    prepare(1 - y_hi)
    shift(1 - y_hi, 0, 8)
    row_a(3)
    row_a(4)
    own_a(2)
    own_b(1, 2, 3, 4)
    shift(1 - y_hi, 8, 16)
    row_a(5)
    row_a(6)
    own_a(3, 4)
    sib_a(1, 2)
    sib_b(1, 2, 3, 4)
    from_w(4, -3, 5)
    from_w(6, 3, 6)
    own_a(5, 6)
    own_b(5, 6)
    sib_a(3, 4)
    from_w(5, -4, 7)
    row_a(7)
    own_a(7)
    own_b(7)
    sib_a(5, 6)
    sib_b(5, 6)
    sib_a(7)
    sib_b(7)

    @pl.loop(0, 2)
    def _(tile):
        at = pl.ds(pl.multiple_of(tile * 896, 128), 896)
        logits[:, at] = lax.dot_general(
            shifted[at, :], weights[...], (((1,), (1,)), ((), ())), preferred_element_type=jnp.float32
        ).T

    sub = lax.broadcasted_iota(jnp.int32, (8, 128), 0)

    def over_group(value, join):
        value = join(value, pltpu.roll(value, 4, 0))
        value = join(value, jnp.where(sub % 2 == 0, pltpu.roll(value, 7, 0), pltpu.roll(value, 1, 0)))
        return join(value, pltpu.roll(value, 64, 1))

    live = lax.broadcasted_iota(jnp.int32, (256, 128), 1) < 64
    last = pl.ds(LIVE - 64, 128)
    logits[:, last] = jnp.where(live, logits[:, last], -3.0e38)

    def peak_of(tile, carry):
        at = pl.ds(pl.multiple_of(tile * 128, 128), 128)
        return jnp.maximum(carry, jnp.max(logits[:, at].reshape(32, 8, 128), axis=0))

    peak = over_group(lax.fori_loop(0, 13, peak_of, jnp.full((8, 128), -3.0e38, jnp.float32)), jnp.maximum)

    def total_of(tile, carry):
        at = pl.ds(pl.multiple_of(tile * 128, 128), 128)
        value = jnp.exp(logits[:, at].reshape(32, 8, 128) - peak[None])
        logits[:, at] = value.reshape(256, 128)
        return carry + jnp.sum(value, axis=0)

    total = over_group(lax.fori_loop(0, 13, total_of, jnp.zeros((8, 128), jnp.float32)), jnp.add)

    stats[y, 0] = peak
    stats[y, 1] = total
    for i in range(3):
        send(stats.at[y], stats.at[y], s_st.at[i], r_st.at[i], y_peers[i])
    for i in range(3):
        landed(stats.at[yat(4 - YPEER[i])], r_st.at[i])
    peaks = [stats[i, 0] for i in range(4)]
    top = jnp.maximum(jnp.maximum(peaks[0], peaks[1]), jnp.maximum(peaks[2], peaks[3]))
    whole = stats[0, 1] * jnp.exp(peaks[0] - top)
    for i in range(1, 4):
        whole = whole + stats[i, 1] * jnp.exp(peaks[i] - top)
    scale = jnp.exp(peak - top) / whole
    llr[core] = top + jnp.log(whole)
    send(llr.at[core], llr.at[core], s_ll, r_ll, sibling)

    @pl.loop(0, 13)
    def _(tile):
        at = pl.ds(pl.multiple_of(tile * 128, 128), 128)
        value = logits[:, at].reshape(32, 8, 128) * scale[None]
        post[:, at] = value.reshape(256, 128).astype(jnp.bfloat16)

    def product(at):
        return jnp.dot(post[...], shifted[:, at], preferred_element_type=jnp.float32)

    def store(at, top_, bottom, width):
        keep = lax.broadcasted_iota(jnp.int32, (256, width), 0) % 8 < 4
        even = jnp.where(keep, top_, pltpu.roll(bottom, 4, 0))
        odd = jnp.where(keep, pltpu.roll(top_, 252, 0), bottom)
        part[:, 0, :, at] = even.reshape(32, 8, width)
        part[:, 1, :, at] = odd.reshape(32, 8, width)

    def trade(at, i):
        send(part.at[pl.ds((1 - core) * 16, 16), :, :, at], sib.at[:, :, :, at], s_d2.at[i], r_d2.at[i], sibling)

    def collect(at, i):
        landed(sib.at[:, :, :, at], r_d2.at[i])

        @pl.loop(0, 16)
        def _(pair):
            row = core * 16 + pair
            part[row, :, :, at] = part[row, :, :, at] + sib[pair, :, :, at]

    sa, sb = pl.ds(0, SCUT), pl.ds(SCUT, SUMW - SCUT)

    def pa(dz, dx, at):
        xx = xat(dx)
        return part.at[core * 16 + zat(dz) * 2 + lax.div(xx, 2), lax.rem(xx, 2), :, at]

    def add(dst, src):
        dst[...] = dst[...] + src[...]

    acols = [pl.ds(0, 896), pl.ds(896, 768)]
    acut = [pl.ds(0, 896), pl.ds(0, 768)]

    def a_away(p, i):
        to = x_up if i % 2 == 0 else x_down
        send(pa(ORDER[i], 2, acols[p]), ax_f.at[p, i, :, acut[p]], s_af.at[p, i], r_af.at[p, i], to)

    def a_near(p, i):
        if i % 2 == 0:
            send(pa(ORDER[i], -1, acols[p]), ax_r.at[p, i, :, acut[p]], s_ar.at[p, i], r_ar.at[p, i], x_down)
        else:
            send(pa(ORDER[i], 1, acols[p]), ax_l.at[p, i, :, acut[p]], s_al.at[p, i], r_al.at[p, i], x_up)

    def a_far(p, i):
        d = ORDER[i]
        landed(ax_f.at[p, i, :, acut[p]], r_af.at[p, i])
        if i % 2 == 0:
            add(ax_f.at[p, i, :, acut[p]], pa(d, 1, acols[p]))
            send(ax_f.at[p, i, :, acut[p]], ax_l.at[p, i, :, acut[p]], s_al.at[p, i], r_al.at[p, i], x_up)
        else:
            add(ax_f.at[p, i, :, acut[p]], pa(d, -1, acols[p]))
            send(ax_f.at[p, i, :, acut[p]], ax_r.at[p, i, :, acut[p]], s_ar.at[p, i], r_ar.at[p, i], x_down)

    def a_sum(p, i):
        own_ = pa(ORDER[i], 0, acols[p])
        landed(ax_l.at[p, i, :, acut[p]], r_al.at[p, i])
        landed(ax_r.at[p, i, :, acut[p]], r_ar.at[p, i])
        own_[...] = own_[...] + ax_l[p, i, :, acut[p]] + ax_r[p, i, :, acut[p]]
        if p == 1 and i in (0, 1, 2):
            send(own_, ae.at[p, i, :, acut[p]], s_ae.at[p, i], r_ae.at[p, i], device(y, core, x, zat(ORDER[i])))
        elif p == 1 and i in (3, 4):
            k = i - 1
            send(own_, ag.at[p, k, :, acut[p]], s_ag.at[p, k], r_ag.at[p, k], device(y, core, x, zat(ORDER[i])))
        elif i < 3:
            send(own_, ae.at[p, i, :, acut[p]], s_ae.at[p, i], r_ae.at[p, i], device(y, core, x, zat((-2, -1, 1)[i])))
        elif i in (5, 6):
            send(own_, ag.at[p, i - 5, :, acut[p]], s_ag.at[p, i - 5], r_ag.at[p, i - 5], device(y, core, x, zat(ORDER[i])))

    def a_join(p):
        ref = pa(-2, 0, acols[p])
        landed(ae.at[p, 0, :, acut[p]], r_ae.at[p, 0])
        landed(ae.at[p, 1, :, acut[p]], r_ae.at[p, 1])
        ref[...] = ref[...] + ae[p, 0, :, acut[p]] + ae[p, 1, :, acut[p]]
        send(ref, ag.at[p, 2, :, acut[p]], s_ag.at[p, 2], r_ag.at[p, 2], device(y, core, x, zat(-2)))
        ref = pa(2, 0, acols[p])
        landed(ae.at[p, 2, :, acut[p]], r_ae.at[p, 2])
        ref[...] = ref[...] + ae[p, 2, :, acut[p]]
        send(ref, ag.at[p, 3, :, acut[p]], s_ag.at[p, 3], r_ag.at[p, 3], device(y, core, x, zat(2)))

    def a_end(p):
        own_ = pa(0, 0, acols[p])
        if p == 1:
            for i in range(3):
                landed(ae.at[p, i, :, acut[p]], r_ae.at[p, i])
            own_[...] = own_[...] + ae[p, 0, :, acut[p]] + (ae[p, 1, :, acut[p]] + ae[p, 2, :, acut[p]])
        for i in range(4):
            landed(ag.at[p, i, :, acut[p]], r_ag.at[p, i])
        own_[...] = own_[...] + ((ag[p, 0, :, acut[p]] + ag[p, 1, :, acut[p]]) + (ag[p, 2, :, acut[p]] + ag[p, 3, :, acut[p]]))

    def pb(dz):
        return part.at[pl.ds(core * 16 + zat(dz) * 2, 2), :, :, sb]

    def b_start():
        for i, (row, step) in enumerate(((4, 2), (3, 1), (-3, -1))):
            send(pb(row), be.at[i], s_be.at[i], r_be.at[i], device(y, core, x, zat(step)))
        for i, step in enumerate((-1, 1)):
            send(pb(step), bg.at[i], s_bg.at[i], r_bg.at[i], device(y, core, x, zat(step)))

    def b_join():
        landed(be.at[0], r_be.at[0])
        landed(be.at[1], r_be.at[1])
        ref = pb(2)
        ref[...] = ref[...] + be[0] + be[1]
        send(ref, bg.at[2], s_bg.at[2], r_bg.at[2], device(y, core, x, zat(2)))
        landed(be.at[2], r_be.at[2])
        ref = pb(-2)
        ref[...] = ref[...] + be[2]
        send(ref, bg.at[3], s_bg.at[3], r_bg.at[3], device(y, core, x, zat(-2)))

    def b_sum():
        for i in range(4):
            landed(bg.at[i], r_bg.at[i])
        ref = pb(0)
        ref[...] = ref[...] + ((bg[0] + bg[1]) + (bg[2] + bg[3]))
        for i in range(3):
            send(pa(0, XPEER[i], sb), bx.at[i], s_bx.at[i], r_bx.at[i], x_peers[i])

    def b_end():
        own_ = pa(0, 0, sb)
        for i in range(3):
            landed(bx.at[i], r_bx.at[i])
        own_[...] = own_[...] + bx[0] + (bx[1] + bx[2])

    def piece(start, width):
        store(
            pl.ds(128 + start, width), product(pl.ds(start, width)), product(pl.ds(FPIX + start, width)), width
        )

    edge = product(pl.ds(2 * FPIX, 128))
    store(pl.ds(0, 128), edge, edge, 128)
    piece(0, 512)
    piece(512, 256)
    trade(acols[0], 0)
    piece(1536, 512)
    trade(sb, 2)
    collect(acols[0], 0)
    for i in range(8):
        a_away(0, i)
    for i in (1, 0, 3, 2):
        a_near(0, i)
    piece(768, 512)
    collect(sb, 2)
    b_start()
    a_far(0, 0)
    a_far(0, 1)
    piece(1280, 256)
    trade(acols[1], 1)
    a_far(0, 2)
    a_far(0, 3)
    a_near(0, 5)
    a_near(0, 4)
    a_far(0, 4)
    a_far(0, 5)
    a_near(0, 7)
    a_near(0, 6)
    a_far(0, 6)
    a_far(0, 7)
    collect(acols[1], 1)
    for i in range(8):
        a_away(1, i)
    for i in (1, 0, 3, 2):
        a_near(1, i)
    for i in range(3):
        a_sum(0, i)
    b_join()
    a_far(1, 0)
    a_far(1, 1)
    a_sum(0, 3)
    a_sum(0, 4)
    a_far(1, 2)
    a_far(1, 3)
    a_near(1, 5)
    a_near(1, 4)
    a_far(1, 4)
    a_far(1, 5)
    a_near(1, 7)
    a_near(1, 6)
    a_sum(0, 5)
    a_sum(0, 6)
    a_join(0)
    a_far(1, 6)
    a_far(1, 7)
    b_sum()
    for i in range(5):
        a_sum(1, i)
    for i in range(5, 8):
        a_sum(1, i)
    a_sum(0, 7)
    b_end()
    a_end(0)
    a_end(1)

    done = part[core * 16 + z * 2 + lax.div(x, 2), lax.rem(x, 2)]
    for r in range(2):
        for k in range(2):
            for c in range(2):
                row, to = 4 * c + 2 * r + k, 4 * r + 2 * k + c
                sums_out[to : to + 1, :] = done[row : row + 1, 128:SUMW]

    landed(llr.at[1 - core], r_ll)
    value = jnp.where(
        lax.broadcasted_iota(jnp.int32, (8, 128), 1) < 32,
        jnp.where(y_hi == 0, llr[0], pltpu.roll(llr[0], 96, 1)),
        jnp.where(y_hi == 1, llr[1], pltpu.roll(llr[1], 32, 1)),
    )
    rest_out[0:1, :] = value[0:1]
    rest_out[1:2, :] = value[2:3]
    for r in range(2):
        rest_out[2 + r : 3 + r, :] = jnp.where(lane == 0, done[2 * r : 2 * r + 1, 0:1], done[2 * r + 1 : 2 * r + 2, 0:1])

    left(pix.at[0], s_pix.at[0])
    left(offs.at[0], s_pix.at[1])
    left(llr.at[0], s_ll)
    for i in range(3):
        left(stats.at[0], s_st.at[i])
        left(gb(0, 0), s_y.at[i])
        left(be.at[0], s_be.at[i])
        left(bx.at[0], s_bx.at[i])
    for i in range(4):
        left(bg.at[0], s_bg.at[i])
    for i in range(7):
        left(ga(0, 0), s_z.at[i])
        left(gb_row(0), s_w.at[i])
    for i in range(8):
        for k in range(3):
            left(ga(0, 0), s_x.at[i, k])
        left(ga_row(0), s_sd.at[i])
        left(gb_row(0), s_se.at[i])
    for p in range(2):
        for i in range(8):
            left(ax_f.at[p, 0, :, acut[p]], s_af.at[p, i])
            left(ax_f.at[p, 0, :, acut[p]], s_al.at[p, i])
            left(ax_f.at[p, 0, :, acut[p]], s_ar.at[p, i])
        for i in range(3):
            left(ae.at[p, 0, :, acut[p]], s_ae.at[p, i])
        for i in range(4):
            left(ag.at[p, 0, :, acut[p]], s_ag.at[p, i])
        left(sib.at[:, :, :, acols[p]], s_d2.at[p])
    left(sib.at[:, :, :, sb], s_d2.at[2])


def local(particles, offsets, ref_maps, inv_sigma2, log_prior, orient):
    f32, bf16 = jnp.float32, jnp.bfloat16
    vmem = pl.BlockSpec(memory_space=pltpu.VMEM)
    smem = pl.BlockSpec(memory_space=pltpu.SMEM)
    dma = pltpu.SemaphoreType.DMA

    def twice(*shape):
        return [dma(shape), dma(shape)] if shape else [dma, dma]

    rest = SUMW - SCUT
    scratch = [
        pltpu.VMEM((64, 2, FPIX), bf16),
        pltpu.VMEM((2, 64, 2, FPIX), bf16),
        pltpu.VMEM((16, PACK), f32),
        pltpu.VMEM((2, ZN, XN, 16, PACK), bf16),
        pltpu.VMEM((2, 2, HALF, FPIX), bf16),
        pltpu.VMEM((2, HALF, 128), jnp.int32),
        pltpu.VMEM((3, HALF, 128), f32),
        pltpu.VMEM((ROWS, WIDTH), bf16),
        pltpu.VMEM((256, WIDTH), bf16),
        pltpu.VMEM((256, ROWS), f32),
        pltpu.VMEM((256, ROWS), bf16),
        pltpu.VMEM((4, 2, 8, 128), f32),
        pltpu.VMEM((32, 2, 8, SUMW), f32),
        pltpu.VMEM((16, 2, 8, SUMW), f32),
        pltpu.VMEM((2, 8, 128), f32),
        pltpu.VMEM((2, 8, 8, 896), f32),
        pltpu.VMEM((2, 8, 8, 896), f32),
        pltpu.VMEM((2, 8, 8, 896), f32),
        pltpu.VMEM((2, 3, 8, 896), f32),
        pltpu.VMEM((2, 4, 8, 896), f32),
        pltpu.VMEM((3, 2, 2, 8, rest), f32),
        pltpu.VMEM((4, 2, 2, 8, rest), f32),
        pltpu.VMEM((3, 8, rest), f32),
    ]
    scratch += [dma((2,))] + twice(2) + twice(3) + twice()
    scratch += twice(7) + twice(8, 3) + twice(8) + twice(3) + twice(7) + twice(8)
    scratch += twice(3) + twice(2, 8) * 3 + twice(2, 3) + twice(2, 4)
    scratch += twice(3) + twice(4) + twice(3)
    hbm = pl.BlockSpec(memory_space=pl.ANY)
    sums, small = pl.pallas_call(
        kernel,
        out_shape=(
            jax.ShapeDtypeStruct((8, FPIX), f32),
            jax.ShapeDtypeStruct((4, 128), f32),
        ),
        in_specs=[smem, smem, smem, vmem, vmem, hbm, hbm],
        out_specs=(vmem, vmem),
        scratch_shapes=scratch,
        compiler_params=pltpu.CompilerParams(
            collective_id=0, has_side_effects=True, vmem_limit_bytes=56 * 1024 * 1024
        ),
    )(orient.T, log_prior, offsets.T, inv_sigma2.reshape(1, FPIX), jnp.asarray(tables()), particles, ref_maps)
    return sums.reshape(2, 2, 1, 2, FPIX), small[2:4, 0:2].reshape(2, 2, 1), small[0:2, 0:64]


def solution(mesh):
    return jax.shard_map(
        local,
        mesh=mesh,
        in_specs=(
            P("dom", None, None),
            P("dom", None),
            P("cls", "dom", None, None),
            P(),
            P("cls"),
            P(None, "dom"),
        ),
        out_specs=(P(None, "cls", "dom", None, None), P(None, "cls", "dom"), P(None, "dom")),
        check_vma=False,
    )
```
